256 devices in a mesh: seq: 32 (over x, y, core), head: 8 (over z).
Axes of the slice: x: 4, y: 4, z: 8, core: 2. Of those that a mesh axis runs over, the one named last changes fastest.
Arguments:
- hidden: bfloat16 [16384, 2048], P('seq', 'head'), may hold values from -8.5 to 8.5
- w_query: bfloat16 [2048, 2048], P(None, 'head'), may hold values from -0.125 to 0.125
- w_key: bfloat16 [2048, 2048], P(None, 'head'), may hold values from -0.125 to 0.125
- w_value: bfloat16 [2048, 4096], P(None, 'head'), may hold values from -0.125 to 0.125
- conv_query: bfloat16 [4, 2048], P(None, 'head'), may hold values from -3 to 3
- conv_key: bfloat16 [4, 2048], P(None, 'head'), may hold values from -3 to 3
- conv_value: bfloat16 [4, 4096], P(None, 'head'), may hold values from -3 to 3
- gate_log: float32 [32, 16384], P('head', 'seq'), may hold values from -2.5 to 0, as said below
- strength: float32 [32, 16384], P('head', 'seq'), may hold values from 0 to 1, as said below
- initial_state: float32 [32, 128, 128], P('head'), may hold values from -24 to 24
Outputs:
- core_out: bfloat16 [16384, 4096], P('seq', 'head')
- block_states: float32 [32, 32, 128, 128], P('seq', 'head')
The draws below stay inside these ranges and needn't reach their ends.
Inputs may be any that keep to these rules, and one draw needn't show every extreme that they name: `gate_log`: negative or zero. `strength`: Positive.
All inputs are finite; a program needn't handle non-finite values.
Results may differ from the reference program's by a relative error of at most 0.015.
Values may be sent and summed in bfloat16 or wider, within the bound.
A program may use at most 128 MiB of HBM per device.

```python
import math
import jax
import jax.numpy as jnp
from jax import lax

D = 2048
VALUE_HEADS = 32
HK = 16
DK = 128
DV = 128
CONV = 4
TOK_DEV = 512
SUB = 128
TOKENS = 16384
N_SEQ = 32


def head_kinds(key, count):
    order = jax.random.permutation(jax.random.fold_in(key, 17), VALUE_HEADS)
    return (order < count).astype(jnp.float32)[:, None]


def stretch_kinds(key):
    shard_count = TOKENS // TOK_DEV
    picks = jax.random.randint(jax.random.fold_in(key, 19), (VALUE_HEADS, shard_count), 0, 5)
    first = jnp.arange(shard_count, dtype=jnp.int32)[None, :] == 0
    flags = jnp.where(first, 0.0, (picks < 2).astype(jnp.float32))
    return jnp.broadcast_to(flags[:, :, None], (VALUE_HEADS, shard_count, TOK_DEV)).reshape(VALUE_HEADS, TOKENS)


def late_half():
    position = jnp.arange(TOKENS, dtype=jnp.int32) % TOK_DEV
    return (position >= TOK_DEV // 2).astype(jnp.float32)[None, :]


def draw_hidden(key, part):
    key = jax.random.fold_in(key, 7)
    random_child_keys = jax.random.split(key, 3)
    common = jnp.clip(jax.random.normal(random_child_keys[0], (1, D), jnp.float32), -3.0, 3.0)
    noise = jnp.clip(jax.random.normal(random_child_keys[1], (TOKENS, D), jnp.float32), -4.0, 4.0)
    amplitude = jax.random.uniform(random_child_keys[2], (TOKENS, 1), jnp.float32, 0.6, 1.2)
    return (noise + amplitude * common).astype(jnp.bfloat16)


def draw_gate_log(key, part):
    count = VALUE_HEADS // 2
    quick_mode = head_kinds(key, count)
    active = stretch_kinds(key) * late_half()
    key = jax.random.fold_in(key, 3)
    random_child_keys = jax.random.split(key, 6)
    fast_rate = jnp.exp(jax.random.uniform(random_child_keys[0], (VALUE_HEADS, 1), jnp.float32, math.log(1.0 / 50.0), math.log(1.0 / 25.0)))
    slow_rate = jnp.exp(jax.random.uniform(random_child_keys[1], (VALUE_HEADS, 1), jnp.float32, math.log(0.1), math.log(0.4))) / TOKENS
    element_scaling = jnp.exp(jax.random.uniform(random_child_keys[2], (VALUE_HEADS, TOKENS), jnp.float32, math.log(0.5), math.log(2.0)))
    shard_count = TOKENS // TOK_DEV
    partition_scaling = jnp.exp(jax.random.uniform(random_child_keys[3], (VALUE_HEADS, shard_count, 1), jnp.float32, math.log(0.5), math.log(2.0)))
    partition_scaling = jnp.broadcast_to(partition_scaling, (VALUE_HEADS, shard_count, TOK_DEV)).reshape(VALUE_HEADS, TOKENS)
    element_positions = jax.random.randint(random_child_keys[4], (VALUE_HEADS, 3, 1), 0, TOKENS)
    group_lengths = jnp.log(jax.random.uniform(random_child_keys[5], (VALUE_HEADS, 3, 1), jnp.float32, 0.5, 0.8))
    sequence_numbers = jnp.arange(TOKENS, dtype=jnp.int32)[None, None, :]
    token_groups = jnp.sum(jnp.where(sequence_numbers == element_positions, group_lengths, 0.0), axis=1)
    quick_portion = fast_rate * element_scaling * (active + (1.0 - active) * 0.01)
    gradual_portion = slow_rate * element_scaling * partition_scaling
    return -(quick_mode * quick_portion + (1.0 - quick_mode) * gradual_portion) + token_groups


def draw_strength(key, part):
    count = VALUE_HEADS // 2
    quick_mode = head_kinds(key, count)
    writing = stretch_kinds(key)
    key = jax.random.fold_in(key, 5)
    random_child_keys = jax.random.split(key, 3)
    block_count = TOKENS // SUB
    fast_beta = jnp.exp(jax.random.uniform(random_child_keys[0], (VALUE_HEADS, TOKENS), jnp.float32, math.log(0.2), math.log(0.9)))
    slow_scale = jnp.exp(jax.random.uniform(random_child_keys[1], (VALUE_HEADS, TOKENS), jnp.float32, math.log(0.6), math.log(1.6)))
    block_level = jnp.exp(jax.random.uniform(random_child_keys[2], (VALUE_HEADS, block_count, 1), jnp.float32, math.log(0.25), math.log(4.0)))
    block_level = jnp.broadcast_to(block_level, (VALUE_HEADS, block_count, SUB)).reshape(VALUE_HEADS, TOKENS)
    slow_beta = slow_scale * block_level * (0.5 * DK / TOKENS)
    quick_portion = fast_beta * (writing + (1.0 - writing) * 0.02)
    return quick_mode * quick_portion + (1.0 - quick_mode) * slow_beta


def steps_of(rng, shape, cuts, low, largest):
    factor_of, own = 1.0, jax.random.fold_in(rng, 6)
    for dim, shards_of in cuts:
        steps = jnp.exp(jax.random.uniform(jax.random.fold_in(own, dim), (shards_of,), jnp.float32, low / len(cuts), largest / len(cuts)))
        factor_of = factor_of * jnp.repeat(steps, shape[dim] // shards_of).reshape([-1 if axis == dim else 1 for axis in range(len(shape))])
    return factor_of


def normal_values(rng, shape, deviation, limit, cuts=(), held_as=jnp.bfloat16):
    entries = deviation * jax.random.normal(rng, shape, jnp.float32)
    if cuts:
        entries = entries * steps_of(rng, shape, cuts, -0.22, 0.18)
    return jnp.clip(entries, -limit, limit).astype(held_as)


def setup_inputs(seed: int = 0) -> dict:
    streams_of = jax.random.split(jax.random.key(seed), 11)
    hidden = draw_hidden(jax.random.fold_in(streams_of[10], 71), 0)
    w_query = normal_values(streams_of[1], (D, HK * DK), D ** -0.5, 0.125, ((1, 8),))
    w_key = normal_values(streams_of[2], (D, HK * DK), D ** -0.5, 0.125, ((1, 8),))
    w_value = normal_values(streams_of[3], (D, VALUE_HEADS * DV), D ** -0.5, 0.125, ((1, 8),))
    conv_query = normal_values(streams_of[4], (CONV, HK * DK), 0.5, 3.0, ((1, 8),))
    conv_key = normal_values(streams_of[5], (CONV, HK * DK), 0.5, 3.0, ((1, 8),))
    conv_value = normal_values(streams_of[6], (CONV, VALUE_HEADS * DV), 0.5, 3.0, ((1, 8),))
    gate_log = draw_gate_log(jax.random.fold_in(streams_of[10], 71), 0)
    strength = draw_strength(jax.random.fold_in(streams_of[10], 71), 0)
    initial_state = normal_values(streams_of[9], (VALUE_HEADS, DK, DV), 4.0, 24.0, ((0, 8),), jnp.float32)
    return dict(hidden=hidden, w_query=w_query, w_key=w_key, w_value=w_value, conv_query=conv_query, conv_key=conv_key, conv_value=conv_value, gate_log=gate_log, strength=strength, initial_state=initial_state)


def conv_silu(inputs, kernel):
    length = kernel.shape[0]
    padded = jnp.concatenate([jnp.zeros((length - 1, inputs.shape[1]), inputs.dtype), inputs], axis=0)
    running = jnp.zeros(inputs.shape, jnp.float32)
    for tap_index in range(length):
        running = running + kernel[tap_index].astype(jnp.float32) * padded[tap_index:tap_index + inputs.shape[0]].astype(jnp.float32)
    return jax.nn.silu(running).astype(jnp.bfloat16)

def unit_heads(inputs, head_count, factor):
    shaped = inputs.reshape(inputs.shape[0], head_count, -1).astype(jnp.float32)
    squares = lax.optimization_barrier(jnp.sum(shaped * shaped, axis=-1, keepdims=True))
    return (shaped / jnp.sqrt(squares + 1e-06) * factor).astype(jnp.bfloat16)

def block_step(state, block):
    highest = lax.Precision.HIGHEST
    query_b, key_b, value_b, log_gates, strengths = block
    queries = jnp.transpose(query_b, (1, 0, 2)).astype(jnp.float32)
    keys_f = jnp.transpose(key_b, (1, 0, 2)).astype(jnp.float32)
    values_f = jnp.transpose(value_b, (1, 0, 2)).astype(jnp.float32)
    log_decay = jnp.cumsum(log_gates, axis=-1)
    retain = jnp.exp(log_decay)
    length = log_gates.shape[-1]
    row_ids = lax.broadcasted_iota(jnp.int32, (length, length), 0)
    col_ids = lax.broadcasted_iota(jnp.int32, (length, length), 1)
    on_or_below = row_ids >= col_ids
    below = row_ids > col_ids
    spread = log_decay[:, :, None] - log_decay[:, None, :]
    decay = jnp.where(on_or_below, jnp.exp(jnp.where(on_or_below, spread, 0.0)), 0.0)
    keyed = jnp.einsum('hta,hav->htv', keys_f, state, precision=highest)
    right_side = strengths[:, :, None] * (values_f - retain[:, :, None] * keyed)
    key_gram = jnp.einsum('hta,hsa->hts', keys_f, keys_f, precision=highest)
    system = jnp.eye(length, dtype=jnp.float32) + jnp.where(below, decay * key_gram, 0.0) * strengths[:, :, None]
    updates = jax.scipy.linalg.solve_triangular(system, right_side, lower=True, unit_diagonal=True)
    query_key = jnp.einsum('hta,hsa->hts', queries, keys_f, precision=highest)
    output = retain[:, :, None] * jnp.einsum('hta,hav->htv', queries, state, precision=highest)
    output = output + jnp.einsum('hts,hsv->htv', decay * query_key, updates, precision=highest)
    to_end = jnp.exp(log_decay[:, -1:] - log_decay)
    state = retain[:, -1:, None] * state + jnp.einsum('hta,ht,htv->hav', keys_f, to_end, updates, precision=highest)
    return (state, jnp.transpose(output, (1, 0, 2)).astype(jnp.bfloat16))

def reference(hidden, w_query, w_key, w_value, conv_query, conv_key, conv_value, gate_log, strength, initial_state):
    q_proj = jnp.dot(hidden.astype(jnp.float32), w_query.astype(jnp.float32), preferred_element_type=jnp.float32).astype(jnp.bfloat16)
    k_proj = jnp.dot(hidden.astype(jnp.float32), w_key.astype(jnp.float32), preferred_element_type=jnp.float32).astype(jnp.bfloat16)
    v_proj = jnp.dot(hidden.astype(jnp.float32), w_value.astype(jnp.float32), preferred_element_type=jnp.float32).astype(jnp.bfloat16)
    q_conv = conv_silu(q_proj, conv_query)
    k_conv = conv_silu(k_proj, conv_key)
    v_conv = conv_silu(v_proj, conv_value)
    q_norm = unit_heads(q_conv, HK, DK ** (-0.5))
    k_norm = unit_heads(k_conv, HK, 1.0)
    per_key = VALUE_HEADS // HK
    q_heads = jnp.repeat(q_norm, per_key, axis=1)
    k_heads = jnp.repeat(k_norm, per_key, axis=1)
    v_heads = v_conv.reshape(TOKENS, VALUE_HEADS, DV)
    count = TOK_DEV // SUB

    def stretches(inputs):
        return inputs.reshape(N_SEQ, count, SUB, inputs.shape[1], inputs.shape[2])
    log_gates = jnp.transpose(gate_log.reshape(VALUE_HEADS, N_SEQ, count, SUB), (1, 2, 0, 3))
    strengths = jnp.transpose(strength.reshape(VALUE_HEADS, N_SEQ, count, SUB), (1, 2, 0, 3))

    def shard_step(state, shard):
        state, outputs = lax.scan(block_step, state, shard)
        return (state, (outputs, state))
    last_state, (outputs, states) = lax.scan(shard_step, initial_state, (stretches(q_heads), stretches(k_heads), stretches(v_heads), log_gates, strengths))
    core_out = outputs.reshape(TOKENS, VALUE_HEADS * DV)
    return (core_out, states)
```

```python
import functools

import jax
import jax.numpy as jnp
from jax import lax
from jax.experimental import pallas as pl
from jax.experimental.pallas import tpu as pltpu
from jax.sharding import PartitionSpec as P

MESH = pl.DeviceIdType.MESH
F32 = jnp.float32
BF16 = jnp.bfloat16
SUB = 128
HALO = 16
LEVELS = (2, 4, 8, 16, 32, 64)
NT = (((1,), (1,)), ((), ()))


def mm(left, right):
    return jnp.dot(left, right, preferred_element_type=F32)


def mm_nt(left, right):
    return lax.dot_general(left, right, NT, preferred_element_type=F32)


def split3(value):
    high = value.astype(BF16).astype(F32)
    mid = (value - high).astype(BF16).astype(F32)
    low = value - high - mid
    row = lax.broadcasted_iota(jnp.int32, (16, SUB), 0)
    tile = jnp.where(row == 0, high, jnp.where(row == 1, mid, jnp.where(row == 2, low, 0.0)))
    return tile.astype(BF16)


def joined3(tile):
    return jnp.sum(tile.astype(F32), axis=0, keepdims=True)


def kernel(
    n_seq,
    n_head,
    hidden_ref,
    wq_ref,
    wk_ref,
    wv_ref,
    cq_ref,
    ck_ref,
    cv_ref,
    gate_hbm,
    beta_hbm,
    init_hbm,
    core_ref,
    closing_ref,
    gbuf,
    own_halo,
    w_ref,
    gate_ref,
    beta_ref,
    init_ref,
    x_ref,
    tap_ref,
    mask_ref,
    state_ref,
    decay_ref,
    partial_ref,
    reach_ref,
    total_ref,
    tx0,
    rx0,
    tx1,
    rx1,
    tx2,
    inc_ref,
    initt_ref,
    local_sem,
    ring_send,
    ring_recv,
    halo_sem,
    pair_sem,
    a_send,
    a_recv,
    b_send,
    b_recv,
):
    tokens = hidden_ref.shape[0]
    width = hidden_ref.shape[1]
    blocks = tokens // SUB
    heads = gate_hbm.shape[0]
    qcols = wq_ref.shape[1]
    n_chip = n_seq // 2
    me_s = lax.axis_index("seq")
    me_h = lax.axis_index("head")
    core = lax.rem(me_s, 2)
    chip = lax.div(me_s, 2)
    partner = me_s + 1 - 2 * core
    right = lax.rem(me_h + 1, n_head)
    left = lax.rem(me_h + n_head - 1, n_head)

    own_halo[...] = jnp.zeros_like(own_halo)
    barrier = pltpu.get_barrier_semaphore()
    for neighbour in (left, right):
        pl.semaphore_signal(
            barrier, inc=1, device_id={"seq": me_s, "head": neighbour}, device_id_type=MESH
        )

    def greet(i, carry):
        @pl.when(i != me_s)
        def _():
            pl.semaphore_signal(
                barrier, inc=1, device_id={"seq": i, "head": me_h}, device_id_type=MESH
            )

        return carry

    lax.fori_loop(0, n_seq, greet, 0)

    loads = []
    for source, target in (
        (wq_ref, w_ref.at[:, pl.ds(0, qcols)]),
        (wk_ref, w_ref.at[:, pl.ds(qcols, qcols)]),
        (wv_ref, w_ref.at[:, pl.ds(2 * qcols, wv_ref.shape[1])]),
        (gate_hbm, gate_ref),
        (beta_hbm, beta_ref),
        (init_hbm, init_ref),
    ):
        loads.append(pltpu.make_async_copy(source, target, local_sem.at[1 + len(loads)]))
        loads[-1].start()

    row = lax.broadcasted_iota(jnp.int32, (SUB, SUB), 0)
    col = lax.broadcasted_iota(jnp.int32, (SUB, SUB), 1)
    for index, size in enumerate(LEVELS):
        here = (lax.div(row, 2 * size) == lax.div(col, 2 * size)) & (
            lax.div(row, size) > lax.div(col, size)
        )
        mask_ref[index] = jnp.where(here, 1.0, 0.0).astype(BF16)
    tap_ref[:, :qcols] = cq_ref[...].astype(F32)
    tap_ref[:, qcols : 2 * qcols] = ck_ref[...].astype(F32)
    tap_ref[:, 2 * qcols :] = cv_ref[...].astype(F32)
    state_ref[...] = jnp.zeros_like(state_ref)
    decay_ref[...] = jnp.ones_like(decay_ref)

    pl.semaphore_wait(barrier, n_seq - 1 + 2)

    halo_copy = pltpu.make_async_remote_copy(
        src_ref=hidden_ref.at[pl.ds(tokens - HALO, HALO)],
        dst_ref=own_halo,
        send_sem=halo_sem.at[0],
        recv_sem=halo_sem.at[1],
        device_id={"seq": lax.rem(me_s + 1, n_seq), "head": me_h},
        device_id_type=MESH,
    )

    @pl.when(me_s < n_seq - 1)
    def _():
        halo_copy.start()

    half = n_head // 2
    part_rows = SUB // 2

    def hop(direction, chunk, part, distance):
        back = distance - 1
        if direction == 0:
            owner, target = lax.rem(me_h + n_head - back, n_head), right
        else:
            owner, target = lax.rem(me_h + back, n_head), left
        if isinstance(chunk, int) and chunk == blocks:
            rows = pl.ds(tokens, HALO)
        else:
            rows = pl.ds(pl.multiple_of(chunk * SUB + part * part_rows, part_rows), part_rows)
        columns = pl.ds(pl.multiple_of(owner * width, width), width)
        place = gbuf.at[rows, columns]
        if distance > 1:
            source = place
        elif isinstance(chunk, int) and chunk == blocks:
            source = own_halo
        else:
            source = hidden_ref.at[rows]
        return pltpu.make_async_remote_copy(
            src_ref=source,
            dst_ref=place,
            send_sem=ring_send.at[direction, chunk, part, back],
            recv_sem=ring_recv.at[direction, chunk, part, back],
            device_id={"seq": me_s, "head": target},
            device_id_type=MESH,
        )

    def used(direction, part, distance):
        return distance < half or (distance == half and part == direction)

    def event(chunk, part, distance):
        for direction in (0, 1):
            if used(direction, part, distance):
                if distance > 1:
                    hop(direction, chunk, part, distance - 1).wait_recv()
                hop(direction, chunk, part, distance).start()

    def arrived(chunk, parts=(0, 1)):
        for part in parts:
            for direction in (0, 1):
                last = half if used(direction, part, half) else half - 1
                if last:
                    hop(direction, chunk, part, last).wait_recv()

    def sent(chunk, parts=(0, 1)):
        for part in parts:
            for direction in (0, 1):
                for distance in range(1, half + 1):
                    if used(direction, part, distance):
                        hop(direction, chunk, part, distance).wait_send()

    split = max(half // 2, 1)
    early, late = range(1, split + 1), range(split + 1, half + 1)

    def ring_events(chunk):
        calls = []
        for k in range(max(len(early), len(late))):
            for part in (0, 1):
                if k < len(late):
                    calls.append((0, part, late[k]))
                if k < len(early):
                    calls.append((1, part, early[k]))

        def make(ahead, part, distance):
            def call():
                @pl.when(chunk + ahead < blocks)
                def _():
                    event(chunk + ahead, part, distance)

            return call

        return [make(*call) for call in calls]

    own_columns = pl.ds(pl.multiple_of(me_h * width, width), width)
    own_copy = pltpu.make_async_copy(
        hidden_ref, gbuf.at[pl.ds(0, tokens), own_columns], local_sem.at[0]
    )
    own_copy.start()
    for distance in early:
        for part in (0, 1):
            event(0, part, distance)

    @pl.when(me_s > 0)
    def _():
        halo_copy.wait_recv()

    gbuf[pl.ds(tokens, HALO), own_columns] = own_halo[...]
    calls = ring_events(0)
    event(blocks, 0, 1)
    for index, call in enumerate(calls):
        call()
        if index % 2 == 1 and index // 2 + 2 <= half:
            event(blocks, 0, index // 2 + 2)
    own_copy.wait()
    for copy in loads:
        copy.wait()
    arrived(blocks, (0,))

    def project(start, size, place, columns=slice(None)):
        rows = gbuf[pl.ds(start, size), :]
        x_ref[pl.ds(place, size), columns] = mm(rows, w_ref[:, columns]).astype(BF16).astype(F32)

    project(tokens, HALO, 0)

    def conv(base, columns):
        total = None
        window = x_ref[pl.ds(base, SUB + HALO), columns]
        for tap in range(4):
            first = HALO - 3 + tap
            term = tap_ref[tap : tap + 1, columns] * window[first : first + SUB]
            total = term if total is None else total + term
        return (total / (1.0 + jnp.exp(-total))).astype(BF16)

    def unit(value, factor):
        value = value.astype(F32)
        squares = jnp.sum(value * value, axis=1, keepdims=True)
        return (value * (lax.rsqrt(squares + 1e-06) * factor)).astype(BF16)

    def block_step(n, carry):
        base = pl.multiple_of(n * SUB, SUB)
        here = pl.ds(base, SUB)
        calls = ring_events(n + 1)

        def service(count=1):
            for _ in range(min(count, len(calls))):
                calls.pop(0)()

        arrived(n)
        for part in range(2):
            service()
            columns = slice(part * 2 * qcols, part * 2 * qcols + 2 * qcols)
            project(base, SUB, pl.multiple_of(base + HALO, HALO), columns)
        service()
        on_or_below = row >= col
        below = row > col
        gates = gate_ref[:, here]
        betas = beta_ref[:, here]
        along = jnp.dot(
            jnp.concatenate([gates, gates], axis=0),
            jnp.where(row <= col, 1.0, 0.0),
            precision=lax.Precision.HIGHEST,
            preferred_element_type=F32,
        )[:heads]
        columns8 = jnp.concatenate([along, betas], axis=0).T
        keys, queries, grams, mixes = [], [], [], []
        for kh in range(qcols // SUB):
            at = slice(SUB * kh, SUB * kh + SUB)
            q = unit(conv(base, at), SUB**-0.5)
            k = unit(conv(base, slice(qcols + SUB * kh, qcols + SUB * kh + SUB)), 1.0)
            both = mm_nt(jnp.concatenate([k, q], axis=0), k)
            keys.append(k)
            queries.append(q.astype(F32))
            grams.append(both[:SUB])
            mixes.append(both[SUB:])
        service()
        keys_t = [k.astype(F32).T for k in keys]
        per_key = heads // len(keys)
        lowers, solved, query_mixes, rights = [], [], [], []
        for h in range(heads):
            kh = h // per_key
            c_col = columns8[:, h : h + 1]
            b_col = columns8[:, heads + h : heads + h + 1]
            spread = c_col - along[h : h + 1, :]
            decay = jnp.exp(jnp.where(on_or_below, spread, -1e30))
            lower = jnp.where(below, decay * grams[kh], 0.0) * b_col
            lowers.append(lower.astype(BF16))
            query_mixes.append((decay * mixes[kh]).astype(BF16))
            first = jnp.where(lax.div(row, 2) == lax.div(col, 2), lower, 0.0)
            solved.append((jnp.where(row == col, 1.0, 0.0) - first).astype(BF16))
            v = conv(base, slice(2 * qcols + SUB * h, 2 * qcols + SUB * h + SUB))
            rights.append(
                jnp.concatenate(
                    [
                        (b_col * v.astype(F32)).astype(BF16),
                        ((b_col * jnp.exp(c_col)) * keys[kh].astype(F32)).astype(BF16),
                    ],
                    axis=1,
                )
            )
        for index in range(len(LEVELS)):
            if index % 2 == 0:
                service()
            halves = [
                mm(t, low * mask_ref[index]).astype(BF16) for t, low in zip(solved, lowers)
            ]
            solved = [t - mm(x, t).astype(BF16) for t, x in zip(solved, halves)]
        service(len(calls))
        updates = [mm(t, r).astype(BF16) for t, r in zip(solved, rights)]
        stacked = []
        for h in range(heads):
            to_end = jnp.exp(along[h : h + 1, SUB - 1 :] - along[h : h + 1, :])
            weighted = (keys_t[h // per_key] * to_end).astype(BF16)
            stacked.append(
                mm(jnp.concatenate([query_mixes[h], weighted], axis=0), updates[h])
            )
        for h in range(heads):
            both = stacked[h]
            retain = jnp.exp(columns8[:, h : h + 1])
            keep = jnp.exp(along[h : h + 1, SUB - 1 :])
            query_eff = retain * queries[h // per_key] - both[:SUB, SUB:]
            offset, correction = both[SUB:, :SUB], both[SUB:, SUB:]
            state = state_ref[h]
            so_far = decay_ref[h, 0:1, 0:1]
            moved = mm(
                jnp.concatenate([query_eff, correction], axis=0).astype(BF16),
                state.astype(BF16),
            )
            at = slice(SUB * h, SUB * h + SUB)
            partial_ref[here, at] = both[:SUB, :SUB] + moved[:SUB, :SUB]
            reach_ref[here, at] = (so_far * query_eff - moved[:SUB, SUB:]).astype(BF16)
            state_ref[h, :, :SUB] = keep * state[:, :SUB] - moved[SUB:, :SUB] + offset
            state_ref[h, :, SUB:] = (
                keep * state[:, SUB:] + so_far * correction - moved[SUB:, SUB:]
            )
            decay_ref[h] = decay_ref[h] * keep
        return carry

    lax.fori_loop(0, blocks, block_step, 0)

    for h in range(heads):
        total_ref[h, :SUB] = state_ref[h, :, SUB:].T
        total_ref[h, SUB:] = state_ref[h, :, :SUB].T
        tx0[h, :SUB] = total_ref[h, :SUB].astype(BF16)
        tx0[h, SUB : SUB + 16] = split3(decay_ref[h, 0:1, :])
        tx0[h, SUB + 16 :] = total_ref[h, SUB:].astype(BF16)
    pair = pltpu.make_async_remote_copy(
        src_ref=tx0,
        dst_ref=rx0,
        send_sem=pair_sem.at[0],
        recv_sem=pair_sem.at[1],
        device_id={"seq": partner, "head": me_h},
        device_id_type=MESH,
    )
    pair.start()
    pair.wait()

    own_heads = heads // 2
    slices = n_chip // heads
    slab = SUB // slices
    for i in range(own_heads):
        h = core * own_heads + i
        mine, other = tx0[h], rx0[h]
        flag = (jnp.zeros((1, 1), jnp.int32) + core) == 0
        early = jnp.where(flag, mine.astype(F32), other.astype(F32))
        late = jnp.where(flag, other.astype(F32), mine.astype(F32))
        g0 = joined3(early[SUB : SUB + 16])
        g1 = joined3(late[SUB : SUB + 16])
        c0, s0 = early[:SUB], early[SUB + 16 :]
        c1, s1 = late[:SUB], late[SUB + 16 :]
        moved = mm(jnp.concatenate([c0, s0], axis=0).astype(BF16), c1.astype(BF16))
        c_new = (g1 * c0 + g0 * c1 - moved[:SUB]).astype(BF16)
        s_new = (g1 * s0 + s1 - moved[SUB:]).astype(BF16)
        g_new = split3(g0 * g1)
        for part in range(slices):
            tx1[i, part, :SUB] = c_new
            tx1[i, part, SUB : SUB + 16] = g_new
            tx1[i, part, SUB + 16 :] = s_new[slab * part : slab * part + slab]

    def job(q):
        part = lax.div(q, heads)
        head = lax.rem(part + q, heads)
        return part, head

    def to_handler(q):
        part, head = job(q)
        return pltpu.make_async_remote_copy(
            src_ref=tx1.at[lax.rem(head, own_heads), part],
            dst_ref=rx1.at[chip],
            send_sem=a_send.at[q],
            recv_sem=a_recv.at[chip],
            device_id={"seq": 2 * q + core, "head": me_h},
            device_id_type=MESH,
        )

    def for_me(q):
        return lax.div(job(q)[1], own_heads) == core

    def send_a(q, carry):
        @pl.when((q != chip) & for_me(q))
        def _():
            to_handler(q).start()

        return carry

    lax.fori_loop(0, n_chip, send_a, 0)
    my_part, my_head = job(chip)
    handling = for_me(chip)

    def from_handler(q):
        part, head = job(q)
        return inc_ref.at[head, pl.ds(pl.multiple_of(part * slab, slab), slab)]

    def hand_on(i, other_core):
        return pltpu.make_async_remote_copy(
            src_ref=tx2.at[i],
            dst_ref=from_handler(chip),
            send_sem=b_send.at[i, other_core],
            recv_sem=b_recv.at[chip],
            device_id={"seq": 2 * i + other_core, "head": me_h},
            device_id_type=MESH,
        )

    @pl.when(handling)
    def _():
        rx1[chip] = tx1[lax.rem(my_head, own_heads), my_part]
        initt_ref[...] = init_ref[my_head].T
        state0 = initt_ref[pl.ds(pl.multiple_of(my_part * slab, slab), slab)]

        def chain(i, state):
            tx2[i] = state
            for other_core in (0, 1):

                @pl.when(2 * i + other_core != me_s)
                def _():
                    hand_on(i, other_core).start()

            @pl.when(i != chip)
            def _():
                pltpu.make_async_remote_copy(
                    src_ref=tx1.at[0, 0],
                    dst_ref=rx1.at[i],
                    send_sem=a_send.at[i],
                    recv_sem=a_recv.at[i],
                    device_id={"seq": partner, "head": me_h},
                    device_id_type=MESH,
                ).wait_recv()

            message = rx1[i]
            moved = mm(state.astype(BF16), message[:SUB])
            keep = joined3(message[SUB : SUB + 16])
            return keep * state - moved + message[SUB + 16 :].astype(F32)

        lax.fori_loop(0, n_chip, chain, state0)
        inc_ref[my_head, pl.ds(pl.multiple_of(my_part * slab, slab), slab)] = tx2[chip]

    def receive(q, carry):
        @pl.when(2 * q + lax.div(job(q)[1], own_heads) != me_s)
        def _():
            pltpu.make_async_remote_copy(
                src_ref=tx2.at[0],
                dst_ref=from_handler(q),
                send_sem=b_send.at[0, 0],
                recv_sem=b_recv.at[q],
                device_id={"seq": partner, "head": me_h},
                device_id_type=MESH,
            ).wait_recv()

        return carry

    lax.fori_loop(0, n_chip, receive, 0)

    for h in range(heads):
        came = inc_ref[h]
        first = rx0[h]
        stepped = (
            joined3(first[SUB : SUB + 16]) * came
            - mm(came.astype(BF16), first[:SUB])
            + first[SUB + 16 :].astype(F32)
        )
        flag = (jnp.zeros((1, 1), jnp.int32) + core) == 0
        came = jnp.where(flag, came, stepped)
        at = slice(SUB * h, SUB * h + SUB)
        short = came.astype(BF16)
        core_ref[:, at] = (partial_ref[:, at] + mm_nt(reach_ref[:, at], short)).astype(BF16)
        total = total_ref[h]
        closing = (
            decay_ref[h, 0:1, :] * came - mm(short, total[:SUB].astype(BF16)) + total[SUB:]
        )
        closing_ref[0, h] = closing.T

    @pl.when(me_s < n_seq - 1)
    def _():
        halo_copy.wait_send()

    def sent_ring(chunk, carry):
        sent(chunk)
        return carry

    lax.fori_loop(0, blocks, sent_ring, 0)
    sent(blocks, (0,))

    def sent_a(q, carry):
        @pl.when((q != chip) & for_me(q))
        def _():
            to_handler(q).wait_send()

        return carry

    lax.fori_loop(0, n_chip, sent_a, 0)

    @pl.when(handling)
    def _():
        def sent_b(i, carry):
            for other_core in (0, 1):

                @pl.when(2 * i + other_core != me_s)
                def _():
                    hand_on(i, other_core).wait_send()

            return carry

        lax.fori_loop(0, n_chip, sent_b, 0)


def solution(mesh):
    n_seq, n_head = mesh.shape["seq"], mesh.shape["head"]
    n_chip = n_seq // 2

    def body(hidden, wq, wk, wv, cq, ck, cv, gate, beta, init):
        tokens, width = hidden.shape
        heads = gate.shape[0]
        columns = wq.shape[1] + wk.shape[1] + wv.shape[1]
        slices = n_chip // heads
        slab = SUB // slices
        blocks = tokens // SUB
        vmem = pl.BlockSpec(memory_space=pltpu.VMEM)
        hbm = pl.BlockSpec(memory_space=pltpu.HBM)
        dma = pltpu.SemaphoreType.DMA
        return pl.pallas_call(
            functools.partial(kernel, n_seq, n_head),
            out_shape=(
                jax.ShapeDtypeStruct((tokens, wv.shape[1]), BF16),
                jax.ShapeDtypeStruct((1,) + init.shape, F32),
            ),
            in_specs=[hbm] * 4 + [vmem] * 3 + [hbm] * 3,
            out_specs=(vmem, vmem),
            scratch_shapes=[
                pltpu.VMEM((tokens + HALO, width * n_head), BF16),
                pltpu.VMEM((HALO, width), BF16),
                pltpu.VMEM((wq.shape[0], columns), BF16),
                pltpu.VMEM(gate.shape, F32),
                pltpu.VMEM(beta.shape, F32),
                pltpu.VMEM(init.shape, F32),
                pltpu.VMEM((tokens + HALO, columns), F32),
                pltpu.VMEM((4, columns), F32),
                pltpu.VMEM((len(LEVELS), SUB, SUB), BF16),
                pltpu.VMEM((heads, SUB, 2 * SUB), F32),
                pltpu.VMEM((heads, 8, SUB), F32),
                pltpu.VMEM((tokens, wv.shape[1]), F32),
                pltpu.VMEM((tokens, wv.shape[1]), BF16),
                pltpu.VMEM((heads, 2 * SUB, SUB), F32),
                pltpu.VMEM((heads, 2 * SUB + 16, SUB), BF16),
                pltpu.VMEM((heads, 2 * SUB + 16, SUB), BF16),
                pltpu.VMEM((heads // 2, slices, SUB + 16 + slab, SUB), BF16),
                pltpu.VMEM((n_chip, SUB + 16 + slab, SUB), BF16),
                pltpu.VMEM((n_chip, slab, SUB), F32),
                pltpu.VMEM((heads, SUB, SUB), F32),
                pltpu.VMEM((SUB, SUB), F32),
                dma((7,)),
                dma((2, blocks + 1, 2, n_head // 2)),
                dma((2, blocks + 1, 2, n_head // 2)),
                dma((2,)),
                dma((2,)),
                dma((n_chip,)),
                dma((n_chip,)),
                dma((n_chip, 2)),
                dma((n_chip,)),
            ],
            compiler_params=pltpu.CompilerParams(
                collective_id=0, has_side_effects=True, vmem_limit_bytes=48 * 2**20
            ),
        )(hidden, wq, wk, wv, cq, ck, cv, gate, beta, init)

    return jax.shard_map(
        body,
        mesh=mesh,
        in_specs=(
            P("seq", "head"),
            P(None, "head"),
            P(None, "head"),
            P(None, "head"),
            P(None, "head"),
            P(None, "head"),
            P(None, "head"),
            P("head", "seq"),
            P("head", "seq"),
            P("head", None, None),
        ),
        out_specs=(P("seq", "head"), P("seq", "head", None, None)),
        check_vma=False,
    )
```

```python
import functools

import jax
import jax.numpy as jnp
from jax import lax
from jax.experimental import pallas as pl
from jax.experimental.pallas import tpu as pltpu
from jax.sharding import PartitionSpec as P

MESH = pl.DeviceIdType.MESH
F32 = jnp.float32
BF16 = jnp.bfloat16
SUB = 128
HALO = 16
LEVELS = (2, 4, 8, 16, 32, 64)
FIRST = (
    (0, 0, 0), (1, 1, 0), (1, 0, 0), (2, 0, 0), (0, 1, 0), (0, 0, 1), (1, 1, 1),
    (1, 0, 1), (3, 0, 0), (0, 1, 1), (0, 0, 2), (3, 1, 0), (1, 0, 2), (2, 0, 1),
    (3, 0, 1), (0, 1, 2), (2, 1, 0), (0, 0, 3), (1, 1, 2), (1, 0, 3), (2, 0, 2),
    (2, 1, 1), (3, 0, 2), (3, 1, 1),
)
BESIDE = ((4, 2, 0, 3), (5, 2, 1, 2), (6, 3, 0, 3), (7, 3, 1, 2))
NT = (((1,), (1,)), ((), ()))


def mm(left, right):
    return jnp.dot(left, right, preferred_element_type=F32)


def mm_nt(left, right):
    return lax.dot_general(left, right, NT, preferred_element_type=F32)


def split3(value):
    high = value.astype(BF16).astype(F32)
    mid = (value - high).astype(BF16).astype(F32)
    low = value - high - mid
    row = lax.broadcasted_iota(jnp.int32, (16, SUB), 0)
    tile = jnp.where(row == 0, high, jnp.where(row == 1, mid, jnp.where(row == 2, low, 0.0)))
    return tile.astype(BF16)


def joined3(tile):
    return jnp.sum(tile.astype(F32), axis=0, keepdims=True)


def kernel(
    n_seq,
    n_head,
    hidden_ref,
    wq_ref,
    wk_ref,
    wv_ref,
    cq_hbm,
    ck_hbm,
    cv_hbm,
    gate_hbm,
    beta_hbm,
    init_hbm,
    core_ref,
    closing_ref,
    gbuf,
    w_ref,
    gate_ref,
    beta_ref,
    init_ref,
    cq_ref,
    ck_ref,
    cv_ref,
    x_ref,
    tap_ref,
    mask_ref,
    state_ref,
    decay_ref,
    decays_ref,
    factor_ref,
    retain_ref,
    beta_full,
    both_full,
    rows_ref,
    partial_ref,
    reach_ref,
    total_ref,
    tx0,
    rx0,
    tx1,
    rx1,
    tx2,
    inc_ref,
    initt_ref,
    local_sem,
    sent_sem,
    ring_recv,
    halo_sem,
    pair_sem,
    a_recv,
    b_recv,
):
    tokens = hidden_ref.shape[0]
    width = hidden_ref.shape[1]
    blocks = tokens // SUB
    heads = gate_hbm.shape[0]
    qcols = wq_ref.shape[1]
    n_chip = n_seq // 2
    me_s = lax.axis_index("seq")
    me_h = lax.axis_index("head")
    core = lax.rem(me_s, 2)
    chip = lax.div(me_s, 2)
    partner = me_s + 1 - 2 * core
    right = lax.rem(me_h + 1, n_head)
    left = lax.rem(me_h + n_head - 1, n_head)

    barrier = pltpu.get_barrier_semaphore()
    for neighbour in (left, right):
        pl.semaphore_signal(
            barrier, inc=1, device_id={"seq": me_s, "head": neighbour}, device_id_type=MESH
        )
    later = lax.rem(me_s + 1, n_seq)
    sooner = lax.rem(me_s + n_seq - 1, n_seq)
    for step in range(1, n_head):
        for other in (later, sooner):
            pl.semaphore_signal(
                barrier,
                inc=1,
                device_id={"seq": other, "head": lax.rem(me_h + step, n_head)},
                device_id_type=MESH,
            )

    def greet(i, carry):
        @pl.when(i != me_s)
        def _():
            pl.semaphore_signal(
                barrier, inc=1, device_id={"seq": i, "head": me_h}, device_id_type=MESH
            )

        return carry

    lax.fori_loop(0, n_seq, greet, 0)

    own_columns = pl.ds(pl.multiple_of(me_h * width, width), width)
    own_copy = pltpu.make_async_copy(
        hidden_ref, gbuf.at[pl.ds(0, tokens), own_columns], local_sem.at[0]
    )
    own_copy.start()
    loads = []
    for source, target in (
        (wq_ref, w_ref.at[:, pl.ds(0, qcols)]),
        (wk_ref, w_ref.at[:, pl.ds(qcols, qcols)]),
        (wv_ref, w_ref.at[:, pl.ds(2 * qcols, wv_ref.shape[1])]),
        (gate_hbm, gate_ref),
        (beta_hbm, beta_ref),
        (init_hbm, init_ref),
        (cq_hbm, cq_ref),
        (ck_hbm, ck_ref),
        (cv_hbm, cv_ref),
    ):
        loads.append(pltpu.make_async_copy(source, target, local_sem.at[1 + len(loads)]))
        loads[-1].start()

    row = lax.broadcasted_iota(jnp.int32, (SUB, SUB), 0)
    col = lax.broadcasted_iota(jnp.int32, (SUB, SUB), 1)
    for index, size in enumerate(LEVELS):
        here = (lax.div(row, 2 * size) == lax.div(col, 2 * size)) & (
            lax.div(row, size) > lax.div(col, size)
        )
        mask_ref[index] = jnp.where(here, 1.0, 0.0).astype(BF16)
    state_ref[...] = jnp.zeros_like(state_ref)
    decay_ref[...] = jnp.ones_like(decay_ref)

    own_copy.wait()
    pl.semaphore_wait(barrier, n_seq - 1 + 2 + 2 * (n_head - 1))

    part_rows = SUB // 2

    def hop(way, chunk, which, back):
        owner = lax.rem(me_h + (n_head - back if way == 0 else back), n_head)
        part = way + which - 2 * way * which
        rows = pl.ds(pl.multiple_of(chunk * SUB + part * part_rows, part_rows), part_rows)
        place = gbuf.at[rows, pl.ds(pl.multiple_of(owner * width, width), width)]
        return pltpu.make_async_remote_copy(
            src_ref=place,
            dst_ref=place,
            send_sem=sent_sem.at[0],
            recv_sem=ring_recv.at[way, 2 * chunk + which, back],
            device_id={"seq": me_s, "head": right if way == 0 else left},
            device_id_type=MESH,
        )

    def event(chunk, which, back):
        for way in (0, 1):
            if isinstance(back, int):
                if back:
                    hop(way, chunk, which, back - 1).wait_recv()
            else:

                @pl.when(back > 0)
                def _():
                    hop(way, chunk, which, back - 1).wait_recv()

            hop(way, chunk, which, back).start()

    def service(pair, stage):
        entries = [entry[1:] for entry in BESIDE if entry[0] == stage]
        if entries:

            @pl.when(pair == 0)
            def _():
                for entry in entries:
                    event(*entry)

    def arrived(chunk):
        for way in (0, 1):
            hop(way, chunk, 0, 3).wait_recv()
            hop(way, chunk, 1, 2).wait_recv()

    def halo_hop(step):
        return pltpu.make_async_remote_copy(
            src_ref=gbuf.at[pl.ds(tokens - HALO, HALO), own_columns],
            dst_ref=gbuf.at[pl.ds(tokens, HALO), own_columns],
            send_sem=sent_sem.at[1],
            recv_sem=halo_sem.at[0],
            device_id={"seq": later, "head": lax.rem(me_h + step, n_head)},
            device_id_type=MESH,
        )

    on_or_below = row >= col
    below = row > col

    def prepare(n):
        at = slice(SUB * n, SUB * n + SUB)
        gates = gate_ref[:, at]
        along = jnp.dot(
            jnp.concatenate([gates, gates], axis=0),
            jnp.where(row <= col, 1.0, 0.0),
            precision=lax.Precision.HIGHEST,
            preferred_element_type=F32,
        )[:heads]
        columns8 = jnp.concatenate([along, beta_ref[:, at]], axis=0).T
        for h in range(heads):
            index = n * heads + h
            c_row, c_end = along[h : h + 1, :], along[h : h + 1, SUB - 1 :]
            c_col = columns8[:, h : h + 1]
            b_col = columns8[:, heads + h : heads + h + 1]
            retain = jnp.exp(c_col)
            decay = jnp.exp(jnp.where(on_or_below, c_col - c_row, -1e30))
            decays_ref[index] = decay
            factor_ref[index] = jnp.where(below, decay, 0.0) * b_col
            retain_ref[index] = jnp.broadcast_to(retain, (SUB, SUB))
            beta_full[index] = jnp.broadcast_to(b_col, (SUB, SUB))
            both_full[index] = jnp.broadcast_to(b_col * retain, (SUB, SUB))
            rows_ref[index, 0:1] = jnp.exp(c_end - c_row)
            rows_ref[index, 1:2] = jnp.broadcast_to(jnp.exp(c_end), (1, SUB))

    halo_bytes = gbuf.at[pl.ds(tokens, HALO)]

    def project(start, size, place, columns=slice(None)):
        rows = gbuf[pl.ds(start, size), :]
        x_ref[pl.ds(place, size), columns] = mm(rows, w_ref[:, columns]).astype(BF16).astype(F32)

    def start_conv():
        tap_ref[:, :qcols] = cq_ref[...].astype(F32)
        tap_ref[:, qcols : 2 * qcols] = ck_ref[...].astype(F32)
        tap_ref[:, 2 * qcols :] = cv_ref[...].astype(F32)
        pltpu.make_async_copy(halo_bytes, halo_bytes, halo_sem.at[0]).wait()
        project(tokens, HALO, 0)

        @pl.when(me_s == 0)
        def _():
            x_ref[:HALO] = jnp.zeros((HALO, x_ref.shape[1]), F32)

    for entry in FIRST[:2]:
        event(*entry)
    for step in range(n_head):
        halo_hop(step).start()
    for copy in loads:
        copy.wait()
    for index, entry in enumerate(FIRST[2:], 2):
        if index in (5, 9, 12, 15):
            prepare((5, 9, 12, 15).index(index))
        if index == 17:
            start_conv()
        event(*entry)
    def conv(base, columns):
        total = None
        window = x_ref[pl.ds(base, SUB + HALO), columns]
        for tap in range(4):
            first = HALO - 3 + tap
            term = tap_ref[tap : tap + 1, columns] * window[first : first + SUB]
            total = term if total is None else total + term
        return (total / (1.0 + jnp.exp(-total))).astype(BF16)

    def unit(value, factor):
        value = value.astype(F32)
        squares = jnp.sum(value * value, axis=1, keepdims=True)
        return (value * (lax.rsqrt(squares + 1e-06) * factor)).astype(BF16)

    per_key = heads // (qcols // SUB)

    def project_block(pair, stage, n):
        base = pl.multiple_of(n * SUB, SUB)
        arrived(n)
        for part in range(2):
            service(pair, stage + part)
            columns = slice(part * 2 * qcols, part * 2 * qcols + 2 * qcols)
            project(base, SUB, pl.multiple_of(base + HALO, HALO), columns)

    def systems(n):
        base = pl.multiple_of(n * SUB, SUB)
        found = []
        for kh in range(qcols // SUB):
            at = slice(SUB * kh, SUB * kh + SUB)
            q = unit(conv(base, at), SUB**-0.5)
            k = unit(conv(base, slice(qcols + SUB * kh, qcols + SUB * kh + SUB)), 1.0)
            both = mm_nt(jnp.concatenate([k, q], axis=0), k)
            k = k.astype(F32)
            k_t = k.T
            for h in range(per_key * kh, per_key * kh + per_key):
                index = n * heads + h
                lower = factor_ref[index] * both[:SUB]
                mix = (decays_ref[index] * both[SUB:]).astype(BF16)
                first = jnp.where(lax.div(row, 2) == lax.div(col, 2), lower, 0.0)
                start = (jnp.where(row == col, 1.0, 0.0) - first).astype(BF16)
                v = conv(base, slice(2 * qcols + SUB * h, 2 * qcols + SUB * h + SUB))
                right_side = jnp.concatenate(
                    [
                        (beta_full[index] * v.astype(F32)).astype(BF16),
                        (both_full[index] * k).astype(BF16),
                    ],
                    axis=1,
                )
                weighted = (k_t * rows_ref[index, 0:1]).astype(BF16)
                query = retain_ref[index] * q.astype(F32)
                found.append(
                    (
                        lower.astype(BF16),
                        start,
                        right_side,
                        jnp.concatenate([mix, weighted], axis=0),
                        query,
                    )
                )
        return found

    def pair_step(pair, carry):
        found = []
        for n in (2 * pair, 2 * pair + 1):
            stage = 3 * (len(found) // heads)
            project_block(pair, stage, n)
            service(pair, stage + 2)
            found += systems(n)
        lowers = [each[0] for each in found]
        solved = [each[1] for each in found]
        for index in range(len(LEVELS)):
            if index % 2 == 0:
                service(pair, 6 + index // 2)
            halves = [
                mm(t, low * mask_ref[index]).astype(BF16) for t, low in zip(solved, lowers)
            ]
            solved = [t - mm(x, t).astype(BF16) for t, x in zip(solved, halves)]
        updates = [mm(t, each[2]).astype(BF16) for t, each in zip(solved, found)]
        stacked = [mm(each[3], u) for u, each in zip(updates, found)]
        for second in range(2):
            n = 2 * pair + second
            here = pl.ds(pl.multiple_of(n * SUB, SUB), SUB)
            for h in range(heads):
                both = stacked[heads * second + h]
                keep = rows_ref[n * heads + h, 1:2]
                query_eff = found[heads * second + h][4] - both[:SUB, SUB:]
                offset, correction = both[SUB:, :SUB], both[SUB:, SUB:]
                state = state_ref[h]
                so_far = decay_ref[h, 0:1]
                moved = mm(
                    jnp.concatenate([query_eff, correction], axis=0).astype(BF16),
                    state.astype(BF16),
                )
                at = slice(SUB * h, SUB * h + SUB)
                partial_ref[here, at] = both[:SUB, :SUB] + moved[:SUB, :SUB]
                reach_ref[here, at] = (so_far * query_eff - moved[:SUB, SUB:]).astype(BF16)
                state_ref[h, :, :SUB] = keep * state[:, :SUB] - moved[SUB:, :SUB] + offset
                state_ref[h, :, SUB:] = (
                    keep * state[:, SUB:] + so_far * correction - moved[SUB:, SUB:]
                )
                decay_ref[h] = decay_ref[h] * keep
        return carry

    lax.fori_loop(0, blocks // 2, pair_step, 0)

    for h in range(heads):
        total_ref[h, :SUB] = state_ref[h, :, SUB:].T
        total_ref[h, SUB:] = state_ref[h, :, :SUB].T
        tx0[h, :SUB] = total_ref[h, :SUB].astype(BF16)
        tx0[h, SUB : SUB + 16] = split3(decay_ref[h, 0:1, :])
        tx0[h, SUB + 16 :] = total_ref[h, SUB:].astype(BF16)
    pair = pltpu.make_async_remote_copy(
        src_ref=tx0,
        dst_ref=rx0,
        send_sem=pair_sem.at[0],
        recv_sem=pair_sem.at[1],
        device_id={"seq": partner, "head": me_h},
        device_id_type=MESH,
    )
    pair.start()
    pair.wait()

    own_heads = heads // 2
    slices = n_chip // heads
    slab = SUB // slices
    for i in range(own_heads):
        h = core * own_heads + i
        mine, other = tx0[h], rx0[h]
        flag = (jnp.zeros((1, 1), jnp.int32) + core) == 0
        early = jnp.where(flag, mine.astype(F32), other.astype(F32))
        late = jnp.where(flag, other.astype(F32), mine.astype(F32))
        g0 = joined3(early[SUB : SUB + 16])
        g1 = joined3(late[SUB : SUB + 16])
        c0, s0 = early[:SUB], early[SUB + 16 :]
        c1, s1 = late[:SUB], late[SUB + 16 :]
        moved = mm(jnp.concatenate([c0, s0], axis=0).astype(BF16), c1.astype(BF16))
        c_new = (g1 * c0 + g0 * c1 - moved[:SUB]).astype(BF16)
        s_new = (g1 * s0 + s1 - moved[SUB:]).astype(BF16)
        g_new = split3(g0 * g1)
        for part in range(slices):
            tx1[i, part, :SUB] = c_new
            tx1[i, part, SUB : SUB + 16] = g_new
            tx1[i, part, SUB + 16 :] = s_new[slab * part : slab * part + slab]

    def job(q):
        part = lax.div(q, heads)
        head = lax.rem(part + q, heads)
        return part, head

    def to_handler(q):
        part, head = job(q)
        return pltpu.make_async_remote_copy(
            src_ref=tx1.at[lax.rem(head, own_heads), part],
            dst_ref=rx1.at[chip],
            send_sem=sent_sem.at[2],
            recv_sem=a_recv.at[chip],
            device_id={"seq": 2 * q + core, "head": me_h},
            device_id_type=MESH,
        )

    def for_me(q):
        return lax.div(job(q)[1], own_heads) == core

    def send_a(k, carry):
        q = chip ^ k

        @pl.when((q != chip) & for_me(q))
        def _():
            to_handler(q).start()

        return carry

    lax.fori_loop(0, n_chip, send_a, 0)
    my_part, my_head = job(chip)
    handling = for_me(chip)

    def from_handler(q):
        part, head = job(q)
        return inc_ref.at[head, pl.ds(pl.multiple_of(part * slab, slab), slab)]

    def hand_on(i, other_core):
        return pltpu.make_async_remote_copy(
            src_ref=tx2.at[i],
            dst_ref=from_handler(chip),
            send_sem=sent_sem.at[3],
            recv_sem=b_recv.at[0],
            device_id={"seq": 2 * i + other_core, "head": me_h},
            device_id_type=MESH,
        )

    @pl.when(handling)
    def _():
        rx1[chip] = tx1[lax.rem(my_head, own_heads), my_part]
        initt_ref[...] = init_ref[my_head].T
        state0 = initt_ref[pl.ds(pl.multiple_of(my_part * slab, slab), slab)]

        def chain(i, state):
            tx2[i] = state
            for other_core in (0, 1):

                @pl.when(2 * i + other_core != me_s)
                def _():
                    hand_on(i, other_core).start()

            @pl.when(i != chip)
            def _():
                pltpu.make_async_remote_copy(
                    src_ref=tx1.at[0, 0],
                    dst_ref=rx1.at[i],
                    send_sem=sent_sem.at[2],
                    recv_sem=a_recv.at[i],
                    device_id={"seq": partner, "head": me_h},
                    device_id_type=MESH,
                ).wait_recv()

            message = rx1[i]
            moved = mm(state.astype(BF16), message[:SUB])
            keep = joined3(message[SUB : SUB + 16])
            return keep * state - moved + message[SUB + 16 :].astype(F32)

        lax.fori_loop(0, n_chip, chain, state0)
        inc_ref[my_head, pl.ds(pl.multiple_of(my_part * slab, slab), slab)] = tx2[chip]

    @pl.when(handling)
    def _():
        b_bytes = partial_ref.at[pl.ds(0, (n_chip - 1) * slab // 2), pl.ds(0, 2 * SUB)]
        pltpu.make_async_copy(b_bytes, b_bytes, b_recv.at[0]).wait()

    @pl.when(jnp.logical_not(handling))
    def _():
        b_bytes = partial_ref.at[pl.ds(0, n_chip * slab // 2), pl.ds(0, 2 * SUB)]
        pltpu.make_async_copy(b_bytes, b_bytes, b_recv.at[0]).wait()

    for h in range(heads):
        came = inc_ref[h]
        first = rx0[h]
        stepped = (
            joined3(first[SUB : SUB + 16]) * came
            - mm(came.astype(BF16), first[:SUB])
            + first[SUB + 16 :].astype(F32)
        )
        flag = (jnp.zeros((1, 1), jnp.int32) + core) == 0
        came = jnp.where(flag, came, stepped)
        at = slice(SUB * h, SUB * h + SUB)
        short = came.astype(BF16)
        core_ref[:, at] = (partial_ref[:, at] + mm_nt(reach_ref[:, at], short)).astype(BF16)
        total = total_ref[h]
        closing = (
            decay_ref[h, 0:1, :] * came - mm(short, total[:SUB].astype(BF16)) + total[SUB:]
        )
        closing_ref[0, h] = closing.T

    ring_bytes = gbuf.at[pl.ds(0, tokens), pl.ds(0, (n_head - 1) * width)]
    pltpu.make_async_copy(ring_bytes, ring_bytes, sent_sem.at[0]).wait()
    pltpu.make_async_copy(halo_bytes, halo_bytes, sent_sem.at[1]).wait()

    messages = n_chip // 2

    @pl.when(handling)
    def _():
        a_bytes = rx1.at[pl.ds(0, messages - 1)]
        pltpu.make_async_copy(a_bytes, a_bytes, sent_sem.at[2]).wait()
        b_bytes = partial_ref.at[pl.ds(0, (n_seq - 1) * slab // 2), pl.ds(0, 2 * SUB)]
        pltpu.make_async_copy(b_bytes, b_bytes, sent_sem.at[3]).wait()

    @pl.when(jnp.logical_not(handling))
    def _():
        a_bytes = rx1.at[pl.ds(0, messages)]
        pltpu.make_async_copy(a_bytes, a_bytes, sent_sem.at[2]).wait()


def solution(mesh):
    n_seq, n_head = mesh.shape["seq"], mesh.shape["head"]
    n_chip = n_seq // 2

    def body(hidden, wq, wk, wv, cq, ck, cv, gate, beta, init):
        tokens, width = hidden.shape
        heads = gate.shape[0]
        columns = wq.shape[1] + wk.shape[1] + wv.shape[1]
        slices = n_chip // heads
        slab = SUB // slices
        blocks = tokens // SUB
        vmem = pl.BlockSpec(memory_space=pltpu.VMEM)
        hbm = pl.BlockSpec(memory_space=pltpu.HBM)
        dma = pltpu.SemaphoreType.DMA
        return pl.pallas_call(
            functools.partial(kernel, n_seq, n_head),
            out_shape=(
                jax.ShapeDtypeStruct((tokens, wv.shape[1]), BF16),
                jax.ShapeDtypeStruct((1,) + init.shape, F32),
            ),
            in_specs=[hbm] * 10,
            out_specs=(vmem, vmem),
            scratch_shapes=[
                pltpu.VMEM((tokens + HALO, width * n_head), BF16),
                pltpu.VMEM((wq.shape[0], columns), BF16),
                pltpu.VMEM(gate.shape, F32),
                pltpu.VMEM(beta.shape, F32),
                pltpu.VMEM(init.shape, F32),
                pltpu.VMEM(cq.shape, BF16),
                pltpu.VMEM(ck.shape, BF16),
                pltpu.VMEM(cv.shape, BF16),
                pltpu.VMEM((tokens + HALO, columns), F32),
                pltpu.VMEM((4, columns), F32),
                pltpu.VMEM((len(LEVELS), SUB, SUB), BF16),
                pltpu.VMEM((heads, SUB, 2 * SUB), F32),
                pltpu.VMEM((heads, 8, SUB), F32),
                pltpu.VMEM((blocks * heads, SUB, SUB), F32),
                pltpu.VMEM((blocks * heads, SUB, SUB), F32),
                pltpu.VMEM((blocks * heads, SUB, SUB), F32),
                pltpu.VMEM((blocks * heads, SUB, SUB), F32),
                pltpu.VMEM((blocks * heads, SUB, SUB), F32),
                pltpu.VMEM((blocks * heads, 8, SUB), F32),
                pltpu.VMEM((tokens, wv.shape[1]), F32),
                pltpu.VMEM((tokens, wv.shape[1]), BF16),
                pltpu.VMEM((heads, 2 * SUB, SUB), F32),
                pltpu.VMEM((heads, 2 * SUB + 16, SUB), BF16),
                pltpu.VMEM((heads, 2 * SUB + 16, SUB), BF16),
                pltpu.VMEM((heads // 2, slices, SUB + 16 + slab, SUB), BF16),
                pltpu.VMEM((n_chip, SUB + 16 + slab, SUB), BF16),
                pltpu.VMEM((n_chip, slab, SUB), F32),
                pltpu.VMEM((heads, SUB, SUB), F32),
                pltpu.VMEM((SUB, SUB), F32),
                dma((10,)),
                dma((4,)),
                dma((2, 2 * blocks, n_head // 2)),
                dma((1,)),
                dma((2,)),
                dma((n_chip,)),
                dma((1,)),
            ],
            compiler_params=pltpu.CompilerParams(
                collective_id=0, has_side_effects=True, vmem_limit_bytes=60 * 2**20
            ),
        )(hidden, wq, wk, wv, cq, ck, cv, gate, beta, init)

    return jax.shard_map(
        body,
        mesh=mesh,
        in_specs=(
            P("seq", "head"),
            P(None, "head"),
            P(None, "head"),
            P(None, "head"),
            P(None, "head"),
            P(None, "head"),
            P(None, "head"),
            P("head", "seq"),
            P("head", "seq"),
            P("head", None, None),
        ),
        out_specs=(P("seq", "head"), P("seq", "head", None, None)),
        check_vma=False,
    )
```

```python
import functools

import jax
import jax.numpy as jnp
from jax import lax
from jax.experimental import pallas as pl
from jax.experimental.pallas import tpu as pltpu
from jax.sharding import PartitionSpec as P

MESH = pl.DeviceIdType.MESH
F32 = jnp.float32
BF16 = jnp.bfloat16
SUB = 128
HALO = 16
LEVELS = (2, 4, 8, 16, 32, 64)
FIRST = (
    (0, 0, 0), (1, 1, 0), (1, 0, 0), (2, 0, 0), (0, 1, 0), (0, 0, 1), (1, 1, 1),
    (1, 0, 1), (3, 0, 0), (0, 1, 1), (0, 0, 2), (3, 1, 0), (1, 0, 2), (2, 0, 1),
    (3, 0, 1), (0, 1, 2), (2, 1, 0), (0, 0, 3), (1, 1, 2), (1, 0, 3), (2, 0, 2),
    (2, 1, 1), (3, 0, 2), (3, 1, 1),
)
BESIDE = ((4, 2, 0, 3), (5, 2, 1, 2), (6, 3, 0, 3), (7, 3, 1, 2))
HALO_AFTER = (5, 10, 15, 20)
NT = (((1,), (1,)), ((), ()))


def mm(left, right):
    return jnp.dot(left, right, preferred_element_type=F32)


def mm_nt(left, right):
    return lax.dot_general(left, right, NT, preferred_element_type=F32)


def split3(value):
    high = value.astype(BF16).astype(F32)
    mid = (value - high).astype(BF16).astype(F32)
    low = value - high - mid
    row = lax.broadcasted_iota(jnp.int32, (16, SUB), 0)
    tile = jnp.where(row == 0, high, jnp.where(row == 1, mid, jnp.where(row == 2, low, 0.0)))
    return tile.astype(BF16)


def joined3(tile):
    return jnp.sum(tile.astype(F32), axis=0, keepdims=True)


def kernel(
    n_seq,
    n_head,
    hidden_ref,
    wq_ref,
    wk_ref,
    wv_ref,
    cq_hbm,
    ck_hbm,
    cv_hbm,
    gate_hbm,
    beta_hbm,
    init_hbm,
    core_ref,
    closing_ref,
    gbuf,
    w_ref,
    gate_ref,
    beta_ref,
    init_ref,
    cq_ref,
    ck_ref,
    cv_ref,
    x_ref,
    tap_ref,
    mask_ref,
    state_ref,
    decay_ref,
    decays_ref,
    factor_ref,
    retain_ref,
    beta_full,
    both_full,
    rows_ref,
    partial_ref,
    reach_ref,
    total_ref,
    tx0,
    rx0,
    tx1,
    rx1,
    tx2,
    inc_ref,
    initt_ref,
    local_sem,
    sent_sem,
    ring_recv,
    halo_sem,
    pair_sem,
    a_recv,
    b_recv,
):
    tokens = hidden_ref.shape[0]
    width = hidden_ref.shape[1]
    blocks = tokens // SUB
    heads = gate_hbm.shape[0]
    qcols = wq_ref.shape[1]
    n_chip = n_seq // 2
    me_s = lax.axis_index("seq")
    me_h = lax.axis_index("head")
    core = lax.rem(me_s, 2)
    chip = lax.div(me_s, 2)
    partner = me_s + 1 - 2 * core
    right = lax.rem(me_h + 1, n_head)
    left = lax.rem(me_h + n_head - 1, n_head)

    barrier = pltpu.get_barrier_semaphore()
    for neighbour in (left, right):
        pl.semaphore_signal(
            barrier, inc=1, device_id={"seq": me_s, "head": neighbour}, device_id_type=MESH
        )
    later = lax.rem(me_s + 1, n_seq)

    def greet(i, carry):
        @pl.when(i != me_s)
        def _():
            pl.semaphore_signal(
                barrier, inc=1, device_id={"seq": i, "head": me_h}, device_id_type=MESH
            )

        return carry

    lax.fori_loop(0, n_seq, greet, 0)

    own_columns = pl.ds(pl.multiple_of(me_h * width, width), width)
    own_copy = pltpu.make_async_copy(
        hidden_ref, gbuf.at[pl.ds(0, tokens), own_columns], local_sem.at[0]
    )
    own_copy.start()
    loads = []
    for source, target in (
        (wq_ref, w_ref.at[:, pl.ds(0, qcols)]),
        (wk_ref, w_ref.at[:, pl.ds(qcols, qcols)]),
        (wv_ref, w_ref.at[:, pl.ds(2 * qcols, wv_ref.shape[1])]),
        (gate_hbm, gate_ref),
        (beta_hbm, beta_ref),
        (init_hbm, init_ref),
        (cq_hbm, cq_ref),
        (ck_hbm, ck_ref),
        (cv_hbm, cv_ref),
    ):
        loads.append(pltpu.make_async_copy(source, target, local_sem.at[1 + len(loads)]))
        loads[-1].start()

    row = lax.broadcasted_iota(jnp.int32, (SUB, SUB), 0)
    col = lax.broadcasted_iota(jnp.int32, (SUB, SUB), 1)
    for index, size in enumerate(LEVELS):
        here = (lax.div(row, 2 * size) == lax.div(col, 2 * size)) & (
            lax.div(row, size) > lax.div(col, size)
        )
        mask_ref[index] = jnp.where(here, 1.0, 0.0).astype(BF16)
    pairs = (lax.div(row, 2) == lax.div(col, 2)) & (row > col)
    mask_ref[len(LEVELS)] = jnp.where(pairs, 1.0, 0.0).astype(BF16)
    mask_ref[len(LEVELS) + 1] = jnp.where(row == col, 1.0, 0.0).astype(BF16)
    state_ref[...] = jnp.zeros_like(state_ref)
    decay_ref[...] = jnp.ones_like(decay_ref)

    own_copy.wait()
    pl.semaphore_wait(barrier, n_seq - 1 + 2)

    part_rows = SUB // 2

    def hop(way, chunk, which, back):
        owner = lax.rem(me_h + (n_head - back if way == 0 else back), n_head)
        part = way + which - 2 * way * which
        rows = pl.ds(pl.multiple_of(chunk * SUB + part * part_rows, part_rows), part_rows)
        place = gbuf.at[rows, pl.ds(pl.multiple_of(owner * width, width), width)]
        return pltpu.make_async_remote_copy(
            src_ref=place,
            dst_ref=place,
            send_sem=sent_sem.at[0],
            recv_sem=ring_recv.at[way, 2 * chunk + which, back],
            device_id={"seq": me_s, "head": right if way == 0 else left},
            device_id_type=MESH,
        )

    def event(chunk, which, back):
        for way in (0, 1):
            if isinstance(back, int):
                if back:
                    hop(way, chunk, which, back - 1).wait_recv()
            else:

                @pl.when(back > 0)
                def _():
                    hop(way, chunk, which, back - 1).wait_recv()

            hop(way, chunk, which, back).start()

    def service(pair, stage):
        entries = [entry[1:] for entry in BESIDE if entry[0] == stage]
        if entries:

            if pair == 0:
                for entry in entries:
                    event(*entry)

    def arrived(chunk):
        for way in (0, 1):
            hop(way, chunk, 0, 3).wait_recv()
            hop(way, chunk, 1, 2).wait_recv()

    halo_first = pltpu.make_async_remote_copy(
        src_ref=gbuf.at[pl.ds(tokens - HALO, HALO), own_columns],
        dst_ref=gbuf.at[pl.ds(tokens, HALO), own_columns],
        send_sem=sent_sem.at[1],
        recv_sem=halo_sem.at[0, n_head // 2],
        device_id={"seq": later, "head": me_h},
        device_id_type=MESH,
    )

    def halo_hop(way, back):
        owner = lax.rem(me_h + (n_head - back if way == 0 else back), n_head)
        place = gbuf.at[
            pl.ds(tokens, HALO), pl.ds(pl.multiple_of(owner * width, width), width)
        ]
        return pltpu.make_async_remote_copy(
            src_ref=place,
            dst_ref=place,
            send_sem=sent_sem.at[1],
            recv_sem=halo_sem.at[way, back],
            device_id={"seq": me_s, "head": right if way == 0 else left},
            device_id_type=MESH,
        )

    def halo_event(back):
        if back == 0:
            halo_first.wait_recv()
        for way in (0, 1):
            if back:
                halo_hop(way, back - 1).wait_recv()
            if back < n_head // 2 - way:
                halo_hop(way, back).start()

    on_or_below = row >= col
    below = row > col

    def prepare(n):
        at = slice(SUB * n, SUB * n + SUB)
        gates = gate_ref[:, at]
        along = jnp.dot(
            jnp.concatenate([gates, gates], axis=0),
            jnp.where(row <= col, 1.0, 0.0),
            precision=lax.Precision.HIGHEST,
            preferred_element_type=F32,
        )[:heads]
        columns8 = jnp.concatenate([along, beta_ref[:, at]], axis=0).T
        for h in range(heads):
            index = n * heads + h
            c_row, c_end = along[h : h + 1, :], along[h : h + 1, SUB - 1 :]
            c_col = columns8[:, h : h + 1]
            b_col = columns8[:, heads + h : heads + h + 1]
            retain = jnp.exp(c_col)
            decay = jnp.exp(jnp.where(on_or_below, c_col - c_row, -1e30))
            decays_ref[index] = decay
            factor_ref[index] = jnp.where(below, decay, 0.0) * b_col
            retain_ref[index] = jnp.broadcast_to(retain, (SUB, SUB))
            beta_full[index] = jnp.broadcast_to(b_col, (SUB, SUB))
            both_full[index] = jnp.broadcast_to(b_col * retain, (SUB, SUB))
            rows_ref[index, 0:1] = jnp.exp(c_end - c_row)
            rows_ref[index, 1:2] = jnp.broadcast_to(jnp.exp(c_end), (1, SUB))

    halo_bytes = gbuf.at[pl.ds(tokens, HALO)]

    def project(start, size, place, columns=slice(None)):
        rows = gbuf[pl.ds(start, size), :]
        x_ref[pl.ds(place, size), columns] = mm(rows, w_ref[:, columns]).astype(BF16).astype(F32)

    def start_conv():
        tap_ref[:, :qcols] = cq_ref[...].astype(F32)
        tap_ref[:, qcols : 2 * qcols] = ck_ref[...].astype(F32)
        tap_ref[:, 2 * qcols :] = cv_ref[...].astype(F32)
        halo_hop(0, n_head // 2 - 1).wait_recv()
        project(tokens, HALO, 0)

        @pl.when(me_s == 0)
        def _():
            x_ref[:HALO] = jnp.zeros((HALO, x_ref.shape[1]), F32)

    for entry in FIRST[:2]:
        event(*entry)
    halo_first.start()
    for copy in loads:
        copy.wait()
    for index, entry in enumerate(FIRST[2:], 2):
        if index in (5, 9, 12, 15):
            prepare((5, 9, 12, 15).index(index))
        event(*entry)
        if index in HALO_AFTER:
            halo_event(HALO_AFTER.index(index))
    def conv(base, columns):
        total = None
        window = x_ref[pl.ds(base, SUB + HALO), columns]
        for tap in range(4):
            first = HALO - 3 + tap
            term = tap_ref[tap : tap + 1, columns] * window[first : first + SUB]
            total = term if total is None else total + term
        return (total * pl.reciprocal(1.0 + jnp.exp(-total), approx=True)).astype(BF16)

    def unit(value, factor):
        value = value.astype(F32)
        squares = jnp.sum(value * value, axis=1, keepdims=True)
        return (value * (lax.rsqrt(squares + 1e-06) * factor)).astype(BF16)

    per_key = heads // (qcols // SUB)

    def project_block(pair, stage, n):
        base = n * SUB
        arrived(n)
        for part in range(2):
            service(pair, stage + part)
            columns = slice(part * 2 * qcols, part * 2 * qcols + 2 * qcols)
            project(base, SUB, base + HALO, columns)

    def systems(n):
        base = n * SUB
        found = []
        for kh in range(qcols // SUB):
            at = slice(SUB * kh, SUB * kh + SUB)
            q = unit(conv(base, at), SUB**-0.5)
            k = unit(conv(base, slice(qcols + SUB * kh, qcols + SUB * kh + SUB)), 1.0)
            both = mm_nt(jnp.concatenate([k, q, mask_ref[len(LEVELS) + 1]], axis=0), k)
            k = k.astype(F32)
            k_t = both[2 * SUB :]
            for h in range(per_key * kh, per_key * kh + per_key):
                index = n * heads + h
                lower = factor_ref[index] * both[:SUB]
                mix = (decays_ref[index] * both[SUB : 2 * SUB]).astype(BF16)
                lower = lower.astype(BF16)
                start = mask_ref[len(LEVELS) + 1] - lower * mask_ref[len(LEVELS)]
                v = conv(base, slice(2 * qcols + SUB * h, 2 * qcols + SUB * h + SUB))
                right_side = jnp.concatenate(
                    [
                        (beta_full[index] * v.astype(F32)).astype(BF16),
                        (both_full[index] * k).astype(BF16),
                    ],
                    axis=1,
                )
                weighted = (k_t * rows_ref[index, 0:1]).astype(BF16)
                query = retain_ref[index] * q.astype(F32)
                found.append(
                    (
                        lower,
                        start,
                        right_side,
                        jnp.concatenate([mix, weighted], axis=0),
                        query,
                    )
                )
        return found

    def pair_step(pair, carry):
        found = []
        for n in (2 * pair, 2 * pair + 1):
            stage = 3 * (len(found) // heads)
            project_block(pair, stage, n)
            if stage == 0 and pair == 0:
                start_conv()
            service(pair, stage + 2)
            found += systems(n)
        lowers = [each[0] for each in found]
        solved = [each[1] for each in found]
        for index in range(len(LEVELS)):
            if index % 2 == 0:
                service(pair, 6 + index // 2)
            halves = [
                mm(t, low * mask_ref[index]).astype(BF16) for t, low in zip(solved, lowers)
            ]
            solved = [t - mm(x, t).astype(BF16) for t, x in zip(solved, halves)]
        updates = [mm(t, each[2]).astype(BF16) for t, each in zip(solved, found)]
        stacked = [mm(each[3], u) for u, each in zip(updates, found)]
        for second in range(2):
            n = 2 * pair + second
            here = pl.ds(n * SUB, SUB)
            for h in range(heads):
                both = stacked[heads * second + h]
                keep = rows_ref[n * heads + h, 1:2]
                query_eff = found[heads * second + h][4] - both[:SUB, SUB:]
                offset, correction = both[SUB:, :SUB], both[SUB:, SUB:]
                state = state_ref[h]
                so_far = decay_ref[h, 0:1]
                moved = mm(
                    jnp.concatenate([query_eff, correction], axis=0).astype(BF16),
                    state.astype(BF16),
                )
                at = slice(SUB * h, SUB * h + SUB)
                partial_ref[here, at] = both[:SUB, :SUB] + moved[:SUB, :SUB]
                reach_ref[here, at] = (so_far * query_eff - moved[:SUB, SUB:]).astype(BF16)
                state_ref[h, :, :SUB] = keep * state[:, :SUB] - moved[SUB:, :SUB] + offset
                state_ref[h, :, SUB:] = (
                    keep * state[:, SUB:] + so_far * correction - moved[SUB:, SUB:]
                )
                decay_ref[h] = decay_ref[h] * keep
        return carry

    for pair in range(blocks // 2):
        pair_step(pair, 0)

    for h in range(heads):
        total_ref[h, :SUB] = state_ref[h, :, SUB:].T
        total_ref[h, SUB:] = state_ref[h, :, :SUB].T
        tx0[h, :SUB] = total_ref[h, :SUB].astype(BF16)
        tx0[h, SUB : SUB + 16] = split3(decay_ref[h, 0:1, :])
        tx0[h, SUB + 16 :] = total_ref[h, SUB:].astype(BF16)
    own_heads = heads // 2

    def swap(which):
        mine = pl.ds((core if which else 1 - core) * own_heads, own_heads)
        return pltpu.make_async_remote_copy(
            src_ref=tx0.at[mine],
            dst_ref=rx0.at[mine],
            send_sem=pair_sem.at[which],
            recv_sem=pair_sem.at[2 + which],
            device_id={"seq": partner, "head": me_h},
            device_id_type=MESH,
        )

    swap(0).start()
    swap(1).start()
    swap(0).wait_recv()

    slices = n_chip // heads
    slab = SUB // slices
    for i in range(own_heads):
        h = core * own_heads + i
        mine, other = tx0[h], rx0[h]
        flag = (jnp.zeros((1, 1), jnp.int32) + core) == 0
        early = jnp.where(flag, mine.astype(F32), other.astype(F32))
        late = jnp.where(flag, other.astype(F32), mine.astype(F32))
        g0 = joined3(early[SUB : SUB + 16])
        g1 = joined3(late[SUB : SUB + 16])
        c0, s0 = early[:SUB], early[SUB + 16 :]
        c1, s1 = late[:SUB], late[SUB + 16 :]
        moved = mm(jnp.concatenate([c0, s0], axis=0).astype(BF16), c1.astype(BF16))
        c_new = (g1 * c0 + g0 * c1 - moved[:SUB]).astype(BF16)
        s_new = (g1 * s0 + s1 - moved[SUB:]).astype(BF16)
        g_new = split3(g0 * g1)
        for part in range(slices):
            tx1[i, part, :SUB] = c_new
            tx1[i, part, SUB : SUB + 16] = g_new
            tx1[i, part, SUB + 16 :] = s_new[slab * part : slab * part + slab]

    def job(q):
        part = lax.div(q, heads)
        head = lax.rem(part + q, heads)
        return part, head

    def to_handler(q):
        part, head = job(q)
        return pltpu.make_async_remote_copy(
            src_ref=tx1.at[lax.rem(head, own_heads), part],
            dst_ref=rx1.at[chip],
            send_sem=sent_sem.at[2],
            recv_sem=a_recv.at[chip],
            device_id={"seq": 2 * q + core, "head": me_h},
            device_id_type=MESH,
        )

    def for_me(q):
        return lax.div(job(q)[1], own_heads) == core

    def send_a(k, carry):
        q = chip ^ k

        @pl.when((q != chip) & for_me(q))
        def _():
            to_handler(q).start()

        return carry

    lax.fori_loop(0, n_chip, send_a, 0)
    my_part, my_head = job(chip)
    handling = for_me(chip)

    def from_handler(q):
        part, head = job(q)
        return inc_ref.at[head, pl.ds(pl.multiple_of(part * slab, slab), slab)]

    def hand_on(i, other_core):
        return pltpu.make_async_remote_copy(
            src_ref=tx2.at[i],
            dst_ref=from_handler(chip),
            send_sem=sent_sem.at[3],
            recv_sem=b_recv.at[0],
            device_id={"seq": 2 * i + other_core, "head": me_h},
            device_id_type=MESH,
        )

    @pl.when(handling)
    def _():
        rx1[chip] = tx1[lax.rem(my_head, own_heads), my_part]
        initt_ref[...] = init_ref[my_head].T
        state0 = initt_ref[pl.ds(pl.multiple_of(my_part * slab, slab), slab)]

        def chain(i, state):
            tx2[i] = state.astype(BF16)
            for other_core in (0, 1):

                @pl.when(2 * i + other_core != me_s)
                def _():
                    hand_on(i, other_core).start()

            @pl.when(i != chip)
            def _():
                pltpu.make_async_remote_copy(
                    src_ref=tx1.at[0, 0],
                    dst_ref=rx1.at[i],
                    send_sem=sent_sem.at[2],
                    recv_sem=a_recv.at[i],
                    device_id={"seq": partner, "head": me_h},
                    device_id_type=MESH,
                ).wait_recv()

            message = rx1[i]
            moved = mm(state.astype(BF16), message[:SUB])
            keep = joined3(message[SUB : SUB + 16])
            return keep * state - moved + message[SUB + 16 :].astype(F32)

        lax.fori_loop(0, n_chip, chain, state0)
        inc_ref[my_head, pl.ds(pl.multiple_of(my_part * slab, slab), slab)] = tx2[chip]

    @pl.when(handling)
    def _():
        b_bytes = reach_ref.at[pl.ds(0, (n_chip - 1) * slab), pl.ds(0, SUB)]
        pltpu.make_async_copy(b_bytes, b_bytes, b_recv.at[0]).wait()

    @pl.when(jnp.logical_not(handling))
    def _():
        b_bytes = inc_ref
        pltpu.make_async_copy(b_bytes, b_bytes, b_recv.at[0]).wait()

    swap(1).wait_recv()
    for h in range(heads):
        came = inc_ref[h].astype(F32)
        first = rx0[h]
        stepped = (
            joined3(first[SUB : SUB + 16]) * came
            - mm(inc_ref[h], first[:SUB])
            + first[SUB + 16 :].astype(F32)
        )
        flag = (jnp.zeros((1, 1), jnp.int32) + core) == 0
        came = jnp.where(flag, came, stepped)
        at = slice(SUB * h, SUB * h + SUB)
        short = came.astype(BF16)
        core_ref[:, at] = (partial_ref[:, at] + mm_nt(reach_ref[:, at], short)).astype(BF16)
        total = total_ref[h]
        closing = (
            decay_ref[h, 0:1, :] * came - mm(short, total[:SUB].astype(BF16)) + total[SUB:]
        )
        closing_ref[0, h] = closing.T

    swap(0).wait_send()
    swap(1).wait_send()
    ring_bytes = gbuf.at[pl.ds(0, tokens), pl.ds(0, (n_head - 1) * width)]
    pltpu.make_async_copy(ring_bytes, ring_bytes, sent_sem.at[0]).wait()
    pltpu.make_async_copy(halo_bytes, halo_bytes, sent_sem.at[1]).wait()

    messages = n_chip // 2

    @pl.when(handling)
    def _():
        a_bytes = rx1.at[pl.ds(0, messages - 1)]
        pltpu.make_async_copy(a_bytes, a_bytes, sent_sem.at[2]).wait()
        b_bytes = gbuf.at[pl.ds(0, (n_seq - 1) * slab // 2), pl.ds(0, 2 * SUB)]
        pltpu.make_async_copy(b_bytes, b_bytes, sent_sem.at[3]).wait()

    @pl.when(jnp.logical_not(handling))
    def _():
        a_bytes = rx1.at[pl.ds(0, messages)]
        pltpu.make_async_copy(a_bytes, a_bytes, sent_sem.at[2]).wait()


def solution(mesh):
    n_seq, n_head = mesh.shape["seq"], mesh.shape["head"]
    n_chip = n_seq // 2

    def body(hidden, wq, wk, wv, cq, ck, cv, gate, beta, init):
        tokens, width = hidden.shape
        heads = gate.shape[0]
        columns = wq.shape[1] + wk.shape[1] + wv.shape[1]
        slices = n_chip // heads
        slab = SUB // slices
        blocks = tokens // SUB
        vmem = pl.BlockSpec(memory_space=pltpu.VMEM)
        hbm = pl.BlockSpec(memory_space=pltpu.HBM)
        dma = pltpu.SemaphoreType.DMA
        return pl.pallas_call(
            functools.partial(kernel, n_seq, n_head),
            out_shape=(
                jax.ShapeDtypeStruct((tokens, wv.shape[1]), BF16),
                jax.ShapeDtypeStruct((1,) + init.shape, F32),
            ),
            in_specs=[hbm] * 10,
            out_specs=(vmem, vmem),
            scratch_shapes=[
                pltpu.VMEM((tokens + HALO, width * n_head), BF16),
                pltpu.VMEM((wq.shape[0], columns), BF16),
                pltpu.VMEM(gate.shape, F32),
                pltpu.VMEM(beta.shape, F32),
                pltpu.VMEM(init.shape, F32),
                pltpu.VMEM(cq.shape, BF16),
                pltpu.VMEM(ck.shape, BF16),
                pltpu.VMEM(cv.shape, BF16),
                pltpu.VMEM((tokens + HALO, columns), F32),
                pltpu.VMEM((4, columns), F32),
                pltpu.VMEM((len(LEVELS) + 2, SUB, SUB), BF16),
                pltpu.VMEM((heads, SUB, 2 * SUB), F32),
                pltpu.VMEM((heads, 8, SUB), F32),
                pltpu.VMEM((blocks * heads, SUB, SUB), F32),
                pltpu.VMEM((blocks * heads, SUB, SUB), F32),
                pltpu.VMEM((blocks * heads, SUB, SUB), F32),
                pltpu.VMEM((blocks * heads, SUB, SUB), F32),
                pltpu.VMEM((blocks * heads, SUB, SUB), F32),
                pltpu.VMEM((blocks * heads, 8, SUB), F32),
                pltpu.VMEM((tokens, wv.shape[1]), F32),
                pltpu.VMEM((tokens, wv.shape[1]), BF16),
                pltpu.VMEM((heads, 2 * SUB, SUB), F32),
                pltpu.VMEM((heads, 2 * SUB + 16, SUB), BF16),
                pltpu.VMEM((heads, 2 * SUB + 16, SUB), BF16),
                pltpu.VMEM((heads // 2, slices, SUB + 16 + slab, SUB), BF16),
                pltpu.VMEM((n_chip, SUB + 16 + slab, SUB), BF16),
                pltpu.VMEM((n_chip, slab, SUB), BF16),
                pltpu.VMEM((heads, SUB, SUB), BF16),
                pltpu.VMEM((SUB, SUB), F32),
                dma((10,)),
                dma((4,)),
                dma((2, 2 * blocks, n_head // 2)),
                dma((2, n_head // 2 + 1)),
                dma((4,)),
                dma((n_chip,)),
                dma((1,)),
            ],
            compiler_params=pltpu.CompilerParams(
                collective_id=0, has_side_effects=True, vmem_limit_bytes=60 * 2**20
            ),
        )(hidden, wq, wk, wv, cq, ck, cv, gate, beta, init)

    return jax.shard_map(
        body,
        mesh=mesh,
        in_specs=(
            P("seq", "head"),
            P(None, "head"),
            P(None, "head"),
            P(None, "head"),
            P(None, "head"),
            P(None, "head"),
            P(None, "head"),
            P("head", "seq"),
            P("head", "seq"),
            P("head", None, None),
        ),
        out_specs=(P("seq", "head"), P("seq", "head", None, None)),
        check_vma=False,
    )
```

```python
import functools

import jax
import jax.numpy as jnp
from jax import lax
from jax.experimental import pallas as pl
from jax.experimental.pallas import tpu as pltpu
from jax.sharding import PartitionSpec as P

MESH = pl.DeviceIdType.MESH
F32 = jnp.float32
BF16 = jnp.bfloat16
SUB = 128
HALO = 16
LEVELS = (2, 4, 8, 16, 32, 64)
FIRST = (
    (0, 0, 0), (0, 1, 0), (1, 0, 0), (2, 1, 0), (3, 0, 0), (2, 0, 0), (0, 0, 1),
    (1, 1, 0), (1, 0, 1), (2, 1, 1), (3, 1, 0), (0, 1, 1), (0, 0, 2), (1, 1, 1),
    (1, 0, 2), (3, 0, 1), (2, 0, 1), (0, 1, 2), (0, 0, 3), (3, 1, 1), (1, 1, 2),
    (1, 0, 3), (2, 0, 2), (3, 0, 2), (2, 1, 2),
)
BESIDE = ((2, 3, 1, 2), (5, 2, 0, 3), (5, 3, 0, 3),)
HALO_AFTER = (5, 10, 15, 20)
NT = (((1,), (1,)), ((), ()))


def mm(left, right):
    return jnp.dot(left, right, preferred_element_type=F32)


def mm_nt(left, right):
    return lax.dot_general(left, right, NT, preferred_element_type=F32)


def split3(value):
    high = value.astype(BF16).astype(F32)
    mid = (value - high).astype(BF16).astype(F32)
    low = value - high - mid
    row = lax.broadcasted_iota(jnp.int32, (16, SUB), 0)
    tile = jnp.where(row == 0, high, jnp.where(row == 1, mid, jnp.where(row == 2, low, 0.0)))
    return tile.astype(BF16)


def joined3(tile):
    return jnp.sum(tile.astype(F32), axis=0, keepdims=True)


def kernel(
    n_seq,
    n_head,
    hidden_ref,
    wq_ref,
    wk_ref,
    wv_ref,
    cq_hbm,
    ck_hbm,
    cv_hbm,
    gate_hbm,
    beta_hbm,
    init_hbm,
    core_ref,
    closing_ref,
    gbuf,
    w_ref,
    gate_ref,
    beta_ref,
    init_ref,
    cq_ref,
    ck_ref,
    cv_ref,
    x_ref,
    tap_ref,
    mask_ref,
    state_ref,
    decay_ref,
    decays_ref,
    factor_ref,
    retain_ref,
    beta_full,
    both_full,
    rows_ref,
    partial_ref,
    reach_ref,
    total_ref,
    tx0,
    rx0,
    tx1,
    rx1,
    tx2,
    inc_ref,
    initt_ref,
    local_sem,
    sent_sem,
    ring_recv,
    halo_sem,
    pair_sem,
    a_recv,
    b_recv,
):
    tokens = hidden_ref.shape[0]
    width = hidden_ref.shape[1]
    blocks = tokens // SUB
    heads = gate_hbm.shape[0]
    qcols = wq_ref.shape[1]
    n_chip = n_seq // 2
    me_s = lax.axis_index("seq")
    me_h = lax.axis_index("head")
    core = lax.rem(me_s, 2)
    chip = lax.div(me_s, 2)
    partner = me_s + 1 - 2 * core
    right = lax.rem(me_h + 1, n_head)
    left = lax.rem(me_h + n_head - 1, n_head)

    barrier = pltpu.get_barrier_semaphore()
    for neighbour in (left, right):
        pl.semaphore_signal(
            barrier, inc=1, device_id={"seq": me_s, "head": neighbour}, device_id_type=MESH
        )
    later = lax.rem(me_s + 1, n_seq)

    def greet(i, carry):
        @pl.when(i != me_s)
        def _():
            pl.semaphore_signal(
                barrier, inc=1, device_id={"seq": i, "head": me_h}, device_id_type=MESH
            )

        return carry

    lax.fori_loop(0, n_seq, greet, 0)

    own_columns = pl.ds(pl.multiple_of(me_h * width, width), width)
    own_copy = pltpu.make_async_copy(
        hidden_ref, gbuf.at[pl.ds(0, tokens), own_columns], local_sem.at[0]
    )
    own_copy.start()
    loads = []
    for source, target in (
        (wq_ref, w_ref.at[:, pl.ds(0, qcols)]),
        (wk_ref, w_ref.at[:, pl.ds(qcols, qcols)]),
        (wv_ref, w_ref.at[:, pl.ds(2 * qcols, wv_ref.shape[1])]),
        (gate_hbm, gate_ref),
        (beta_hbm, beta_ref),
        (init_hbm, init_ref),
        (cq_hbm, cq_ref),
        (ck_hbm, ck_ref),
        (cv_hbm, cv_ref),
    ):
        loads.append(pltpu.make_async_copy(source, target, local_sem.at[1 + len(loads)]))
        loads[-1].start()

    row = lax.broadcasted_iota(jnp.int32, (SUB, SUB), 0)
    col = lax.broadcasted_iota(jnp.int32, (SUB, SUB), 1)
    for index, size in enumerate(LEVELS):
        here = (lax.div(row, 2 * size) == lax.div(col, 2 * size)) & (
            lax.div(row, size) > lax.div(col, size)
        )
        mask_ref[index] = jnp.where(here, 1.0, 0.0).astype(BF16)
    pairs = (lax.div(row, 2) == lax.div(col, 2)) & (row > col)
    mask_ref[len(LEVELS)] = jnp.where(pairs, 1.0, 0.0).astype(BF16)
    mask_ref[len(LEVELS) + 1] = jnp.where(row == col, 1.0, 0.0).astype(BF16)
    state_ref[...] = jnp.zeros_like(state_ref)
    decay_ref[...] = jnp.ones_like(decay_ref)

    own_copy.wait()
    pl.semaphore_wait(barrier, n_seq - 1 + 2)

    part_rows = SUB // 2

    def hop(way, chunk, which, back):
        owner = lax.rem(me_h + (n_head - back if way == 0 else back), n_head)
        part = way + which - 2 * way * which
        rows = pl.ds(pl.multiple_of(chunk * SUB + part * part_rows, part_rows), part_rows)
        place = gbuf.at[rows, pl.ds(pl.multiple_of(owner * width, width), width)]
        return pltpu.make_async_remote_copy(
            src_ref=place,
            dst_ref=place,
            send_sem=sent_sem.at[0],
            recv_sem=ring_recv.at[way, 2 * chunk + which, back],
            device_id={"seq": me_s, "head": right if way == 0 else left},
            device_id_type=MESH,
        )

    def event(chunk, which, back):
        for way in (0, 1):
            if isinstance(back, int):
                if back:
                    hop(way, chunk, which, back - 1).wait_recv()
            else:

                @pl.when(back > 0)
                def _():
                    hop(way, chunk, which, back - 1).wait_recv()

            hop(way, chunk, which, back).start()

    def service(pair, stage):
        entries = [entry[1:] for entry in BESIDE if entry[0] == stage]
        if entries:

            if pair == 0:
                for entry in entries:
                    event(*entry)

    def arrived(chunk):
        for way in (0, 1):
            hop(way, chunk, 0, 3).wait_recv()
            hop(way, chunk, 1, 2).wait_recv()

    halo_first = pltpu.make_async_remote_copy(
        src_ref=gbuf.at[pl.ds(tokens - HALO, HALO), own_columns],
        dst_ref=gbuf.at[pl.ds(tokens, HALO), own_columns],
        send_sem=sent_sem.at[1],
        recv_sem=halo_sem.at[0, n_head // 2],
        device_id={"seq": later, "head": me_h},
        device_id_type=MESH,
    )

    def halo_hop(way, back):
        owner = lax.rem(me_h + (n_head - back if way == 0 else back), n_head)
        place = gbuf.at[
            pl.ds(tokens, HALO), pl.ds(pl.multiple_of(owner * width, width), width)
        ]
        return pltpu.make_async_remote_copy(
            src_ref=place,
            dst_ref=place,
            send_sem=sent_sem.at[1],
            recv_sem=halo_sem.at[way, back],
            device_id={"seq": me_s, "head": right if way == 0 else left},
            device_id_type=MESH,
        )

    def halo_event(back):
        if back == 0:
            halo_first.wait_recv()
        for way in (0, 1):
            if back:
                halo_hop(way, back - 1).wait_recv()
            if back < n_head // 2 - way:
                halo_hop(way, back).start()

    on_or_below = row >= col
    below = row > col

    def prepare(n):
        at = slice(SUB * n, SUB * n + SUB)
        gates = gate_ref[:, at]
        along = jnp.dot(
            jnp.concatenate([gates, gates], axis=0),
            jnp.where(row <= col, 1.0, 0.0),
            precision=lax.Precision.HIGHEST,
            preferred_element_type=F32,
        )[:heads]
        columns8 = jnp.concatenate([along, beta_ref[:, at]], axis=0).T
        for h in range(heads):
            index = n * heads + h
            c_row, c_end = along[h : h + 1, :], along[h : h + 1, SUB - 1 :]
            c_col = columns8[:, h : h + 1]
            b_col = columns8[:, heads + h : heads + h + 1]
            retain = jnp.exp(c_col)
            decay = jnp.exp(jnp.where(on_or_below, c_col - c_row, -1e30))
            decays_ref[index] = decay
            factor_ref[index] = jnp.where(below, decay, 0.0) * b_col
            retain_ref[index] = jnp.broadcast_to(retain, (SUB, SUB))
            beta_full[index] = jnp.broadcast_to(b_col, (SUB, SUB))
            both_full[index] = jnp.broadcast_to(b_col * retain, (SUB, SUB))
            rows_ref[index, 0:1] = jnp.exp(c_end - c_row)
            rows_ref[index, 1:2] = jnp.broadcast_to(jnp.exp(c_end), (1, SUB))

    halo_bytes = gbuf.at[pl.ds(tokens, HALO)]

    def project(start, size, place, columns=slice(None)):
        rows = gbuf[pl.ds(start, size), :]
        x_ref[pl.ds(place, size), columns] = mm(rows, w_ref[:, columns]).astype(BF16).astype(F32)

    def owner_columns(steps):
        return [
            pl.ds(pl.multiple_of(lax.rem(me_h + step, n_head) * width, width), width)
            for step in steps
        ]

    def gathered(start, size, columns):
        return jnp.concatenate([gbuf[pl.ds(start, size), c] for c in columns], axis=1)

    def weights(owners, columns):
        return jnp.concatenate([w_ref[c, columns] for c in owners], axis=0)

    NEAR, FAR = (0, 1, n_head - 1), tuple(range(2, n_head - 1))

    def project_near(n):
        owners = owner_columns(NEAR)
        rows = gathered(n * SUB, SUB, owners)
        x_ref[pl.ds(n * SUB + HALO, SUB), :] = mm(rows, weights(owners, slice(None)))

    def project_far(start, place, columns):
        owners = owner_columns(FAR)
        total = x_ref[pl.ds(place, SUB), columns] + mm(
            gathered(start, SUB, owners), weights(owners, columns)
        )
        x_ref[pl.ds(place, SUB), columns] = total.astype(BF16).astype(F32)

    def start_conv():
        tap_ref[:, :qcols] = cq_ref[...].astype(F32)
        tap_ref[:, qcols : 2 * qcols] = ck_ref[...].astype(F32)
        tap_ref[:, 2 * qcols :] = cv_ref[...].astype(F32)
        halo_hop(0, n_head // 2 - 1).wait_recv()
        project(tokens, HALO, 0)

        @pl.when(me_s == 0)
        def _():
            x_ref[:HALO] = jnp.zeros((HALO, x_ref.shape[1]), F32)

    for entry in FIRST[:2]:
        event(*entry)
    halo_first.start()
    for copy in loads:
        copy.wait()
    for index, entry in enumerate(FIRST[2:], 2):
        if index in (5, 9, 12, 15):
            prepare((5, 9, 12, 15).index(index))
        event(*entry)
        for n in range(blocks):
            if index == max(FIRST.index((n, 0, 1)), FIRST.index((n, 1, 1))):
                project_near(n)
        if index in HALO_AFTER:
            halo_event(HALO_AFTER.index(index))
    def conv(base, columns):
        total = None
        window = x_ref[pl.ds(base, SUB + HALO), columns]
        for tap in range(4):
            first = HALO - 3 + tap
            term = tap_ref[tap : tap + 1, columns] * window[first : first + SUB]
            total = term if total is None else total + term
        return (total * pl.reciprocal(1.0 + jnp.exp(-total), approx=True)).astype(BF16)

    def unit(value, factor):
        value = value.astype(F32)
        squares = jnp.sum(value * value, axis=1, keepdims=True)
        return (value * (lax.rsqrt(squares + 1e-06) * factor)).astype(BF16)

    per_key = heads // (qcols // SUB)

    def project_block(pair, stage, n):
        base = n * SUB
        arrived(n)
        for part in range(2):
            service(pair, stage + part)
            columns = slice(part * 2 * qcols, part * 2 * qcols + 2 * qcols)
            project_far(base, base + HALO, columns)

    def systems(n):
        base = n * SUB
        found = []
        for kh in range(qcols // SUB):
            at = slice(SUB * kh, SUB * kh + SUB)
            q = unit(conv(base, at), SUB**-0.5)
            k = unit(conv(base, slice(qcols + SUB * kh, qcols + SUB * kh + SUB)), 1.0)
            both = mm_nt(jnp.concatenate([k, q, mask_ref[len(LEVELS) + 1]], axis=0), k)
            k = k.astype(F32)
            k_t = both[2 * SUB :]
            for h in range(per_key * kh, per_key * kh + per_key):
                index = n * heads + h
                lower = factor_ref[index] * both[:SUB]
                mix = (decays_ref[index] * both[SUB : 2 * SUB]).astype(BF16)
                lower = lower.astype(BF16)
                start = mask_ref[len(LEVELS) + 1] - lower * mask_ref[len(LEVELS)]
                v = conv(base, slice(2 * qcols + SUB * h, 2 * qcols + SUB * h + SUB))
                right_side = jnp.concatenate(
                    [
                        (beta_full[index] * v.astype(F32)).astype(BF16),
                        (both_full[index] * k).astype(BF16),
                    ],
                    axis=1,
                )
                weighted = (k_t * rows_ref[index, 0:1]).astype(BF16)
                query = retain_ref[index] * q.astype(F32)
                found.append(
                    (
                        lower,
                        start,
                        right_side,
                        jnp.concatenate([mix, weighted], axis=0),
                        query,
                    )
                )
        return found

    def pair_step(pair, carry):
        found = []
        for n in (2 * pair, 2 * pair + 1):
            stage = 3 * (len(found) // heads)
            project_block(pair, stage, n)
            if stage == 0 and pair == 0:
                start_conv()
            service(pair, stage + 2)
            found += systems(n)
        lowers = [each[0] for each in found]
        solved = [each[1] for each in found]
        for index in range(len(LEVELS)):
            if index % 2 == 0:
                service(pair, 6 + index // 2)
            halves = [
                mm(t, low * mask_ref[index]).astype(BF16) for t, low in zip(solved, lowers)
            ]
            solved = [t - mm(x, t).astype(BF16) for t, x in zip(solved, halves)]
        updates = [mm(t, each[2]).astype(BF16) for t, each in zip(solved, found)]
        stacked = [mm(each[3], u) for u, each in zip(updates, found)]
        for second in range(2):
            n = 2 * pair + second
            here = pl.ds(n * SUB, SUB)
            for h in range(heads):
                both = stacked[heads * second + h]
                keep = rows_ref[n * heads + h, 1:2]
                query_eff = found[heads * second + h][4] - both[:SUB, SUB:]
                offset, correction = both[SUB:, :SUB], both[SUB:, SUB:]
                state = state_ref[h]
                so_far = decay_ref[h, 0:1]
                moved = mm(
                    jnp.concatenate([query_eff, correction], axis=0).astype(BF16),
                    state.astype(BF16),
                )
                at = slice(SUB * h, SUB * h + SUB)
                partial_ref[here, at] = both[:SUB, :SUB] + moved[:SUB, :SUB]
                reach_ref[here, at] = (so_far * query_eff - moved[:SUB, SUB:]).astype(BF16)
                state_ref[h, :, :SUB] = keep * state[:, :SUB] - moved[SUB:, :SUB] + offset
                state_ref[h, :, SUB:] = (
                    keep * state[:, SUB:] + so_far * correction - moved[SUB:, SUB:]
                )
                decay_ref[h] = decay_ref[h] * keep
        return carry

    for pair in range(blocks // 2):
        pair_step(pair, 0)

    for h in range(heads):
        total_ref[h, :SUB] = state_ref[h, :, SUB:].T
        total_ref[h, SUB:] = state_ref[h, :, :SUB].T
        tx0[h, :SUB] = total_ref[h, :SUB].astype(BF16)
        tx0[h, SUB : SUB + 16] = split3(decay_ref[h, 0:1, :])
        tx0[h, SUB + 16 :] = total_ref[h, SUB:].astype(BF16)
    own_heads = heads // 2

    def swap(which):
        mine = pl.ds((core if which else 1 - core) * own_heads, own_heads)
        return pltpu.make_async_remote_copy(
            src_ref=tx0.at[mine],
            dst_ref=rx0.at[mine],
            send_sem=pair_sem.at[which],
            recv_sem=pair_sem.at[2 + which],
            device_id={"seq": partner, "head": me_h},
            device_id_type=MESH,
        )

    swap(0).start()
    swap(1).start()
    swap(0).wait_recv()

    slices = n_chip // heads
    slab = SUB // slices
    def job(q):
        part = lax.div(q, heads)
        head = lax.rem(part + q, heads)
        return part, head

    def to_handler(q):
        part, head = job(q)
        return pltpu.make_async_remote_copy(
            src_ref=tx1.at[lax.rem(head, own_heads), part],
            dst_ref=rx1.at[chip],
            send_sem=sent_sem.at[2],
            recv_sem=a_recv.at[chip],
            device_id={"seq": 2 * q + core, "head": me_h},
            device_id_type=MESH,
        )

    def for_me(q):
        return lax.div(job(q)[1], own_heads) == core

    def send_a(i, k, carry):
        q = chip ^ k

        @pl.when((q != chip) & (job(q)[1] == core * own_heads + i))
        def _():
            to_handler(q).start()

        return carry

    for i in range(own_heads):
        h = core * own_heads + i
        mine, other = tx0[h], rx0[h]
        flag = (jnp.zeros((1, 1), jnp.int32) + core) == 0
        early = jnp.where(flag, mine.astype(F32), other.astype(F32))
        late = jnp.where(flag, other.astype(F32), mine.astype(F32))
        g0 = joined3(early[SUB : SUB + 16])
        g1 = joined3(late[SUB : SUB + 16])
        c0, s0 = early[:SUB], early[SUB + 16 :]
        c1, s1 = late[:SUB], late[SUB + 16 :]
        moved = mm(jnp.concatenate([c0, s0], axis=0).astype(BF16), c1.astype(BF16))
        c_new = (g1 * c0 + g0 * c1 - moved[:SUB]).astype(BF16)
        s_new = (g1 * s0 + s1 - moved[SUB:]).astype(BF16)
        g_new = split3(g0 * g1)
        for part in range(slices):
            tx1[i, part, :SUB] = c_new
            tx1[i, part, SUB : SUB + 16] = g_new
            tx1[i, part, SUB + 16 :] = s_new[slab * part : slab * part + slab]
        lax.fori_loop(0, n_chip, functools.partial(send_a, i), 0)

    my_part, my_head = job(chip)
    handling = for_me(chip)

    def from_handler(q):
        part, head = job(q)
        return inc_ref.at[head, pl.ds(pl.multiple_of(part * slab, slab), slab)]

    def hand_on(i, other_core):
        return pltpu.make_async_remote_copy(
            src_ref=tx2.at[i],
            dst_ref=from_handler(chip),
            send_sem=sent_sem.at[3],
            recv_sem=b_recv.at[0],
            device_id={"seq": 2 * i + other_core, "head": me_h},
            device_id_type=MESH,
        )

    @pl.when(handling)
    def _():
        rx1[chip] = tx1[lax.rem(my_head, own_heads), my_part]
        initt_ref[...] = init_ref[my_head].T
        state0 = initt_ref[pl.ds(pl.multiple_of(my_part * slab, slab), slab)]

        def chain(i, state):
            tx2[i] = state.astype(BF16)
            for other_core in (0, 1):

                @pl.when(2 * i + other_core != me_s)
                def _():
                    hand_on(i, other_core).start()

            @pl.when(i != chip)
            def _():
                pltpu.make_async_remote_copy(
                    src_ref=tx1.at[0, 0],
                    dst_ref=rx1.at[i],
                    send_sem=sent_sem.at[2],
                    recv_sem=a_recv.at[i],
                    device_id={"seq": partner, "head": me_h},
                    device_id_type=MESH,
                ).wait_recv()

            message = rx1[i]
            moved = mm(state.astype(BF16), message[:SUB])
            keep = joined3(message[SUB : SUB + 16])
            return keep * state - moved + message[SUB + 16 :].astype(F32)

        lax.fori_loop(0, n_chip, chain, state0)
        inc_ref[my_head, pl.ds(pl.multiple_of(my_part * slab, slab), slab)] = tx2[chip]

    @pl.when(handling)
    def _():
        b_bytes = reach_ref.at[pl.ds(0, (n_chip - 1) * slab), pl.ds(0, SUB)]
        pltpu.make_async_copy(b_bytes, b_bytes, b_recv.at[0]).wait()

    @pl.when(jnp.logical_not(handling))
    def _():
        b_bytes = inc_ref
        pltpu.make_async_copy(b_bytes, b_bytes, b_recv.at[0]).wait()

    swap(1).wait_recv()
    for h in range(heads):
        came = inc_ref[h].astype(F32)
        first = rx0[h]
        stepped = (
            joined3(first[SUB : SUB + 16]) * came
            - mm(inc_ref[h], first[:SUB])
            + first[SUB + 16 :].astype(F32)
        )
        flag = (jnp.zeros((1, 1), jnp.int32) + core) == 0
        came = jnp.where(flag, came, stepped)
        at = slice(SUB * h, SUB * h + SUB)
        short = came.astype(BF16)
        core_ref[:, at] = (partial_ref[:, at] + mm_nt(reach_ref[:, at], short)).astype(BF16)
        total = total_ref[h]
        closing = (
            decay_ref[h, 0:1, :] * came - mm(short, total[:SUB].astype(BF16)) + total[SUB:]
        )
        closing_ref[0, h] = closing.T

    swap(0).wait_send()
    swap(1).wait_send()
    ring_bytes = gbuf.at[pl.ds(0, tokens), pl.ds(0, (n_head - 1) * width)]
    pltpu.make_async_copy(ring_bytes, ring_bytes, sent_sem.at[0]).wait()
    pltpu.make_async_copy(halo_bytes, halo_bytes, sent_sem.at[1]).wait()

    messages = n_chip // 2

    @pl.when(handling)
    def _():
        a_bytes = rx1.at[pl.ds(0, messages - 1)]
        pltpu.make_async_copy(a_bytes, a_bytes, sent_sem.at[2]).wait()
        b_bytes = gbuf.at[pl.ds(0, (n_seq - 1) * slab // 2), pl.ds(0, 2 * SUB)]
        pltpu.make_async_copy(b_bytes, b_bytes, sent_sem.at[3]).wait()

    @pl.when(jnp.logical_not(handling))
    def _():
        a_bytes = rx1.at[pl.ds(0, messages)]
        pltpu.make_async_copy(a_bytes, a_bytes, sent_sem.at[2]).wait()


def solution(mesh):
    n_seq, n_head = mesh.shape["seq"], mesh.shape["head"]
    n_chip = n_seq // 2

    def body(hidden, wq, wk, wv, cq, ck, cv, gate, beta, init):
        tokens, width = hidden.shape
        heads = gate.shape[0]
        columns = wq.shape[1] + wk.shape[1] + wv.shape[1]
        slices = n_chip // heads
        slab = SUB // slices
        blocks = tokens // SUB
        vmem = pl.BlockSpec(memory_space=pltpu.VMEM)
        hbm = pl.BlockSpec(memory_space=pltpu.HBM)
        dma = pltpu.SemaphoreType.DMA
        return pl.pallas_call(
            functools.partial(kernel, n_seq, n_head),
            out_shape=(
                jax.ShapeDtypeStruct((tokens, wv.shape[1]), BF16),
                jax.ShapeDtypeStruct((1,) + init.shape, F32),
            ),
            in_specs=[hbm] * 10,
            out_specs=(vmem, vmem),
            scratch_shapes=[
                pltpu.VMEM((tokens + HALO, width * n_head), BF16),
                pltpu.VMEM((wq.shape[0], columns), BF16),
                pltpu.VMEM(gate.shape, F32),
                pltpu.VMEM(beta.shape, F32),
                pltpu.VMEM(init.shape, F32),
                pltpu.VMEM(cq.shape, BF16),
                pltpu.VMEM(ck.shape, BF16),
                pltpu.VMEM(cv.shape, BF16),
                pltpu.VMEM((tokens + HALO, columns), F32),
                pltpu.VMEM((4, columns), F32),
                pltpu.VMEM((len(LEVELS) + 2, SUB, SUB), BF16),
                pltpu.VMEM((heads, SUB, 2 * SUB), F32),
                pltpu.VMEM((heads, 8, SUB), F32),
                pltpu.VMEM((blocks * heads, SUB, SUB), F32),
                pltpu.VMEM((blocks * heads, SUB, SUB), F32),
                pltpu.VMEM((blocks * heads, SUB, SUB), F32),
                pltpu.VMEM((blocks * heads, SUB, SUB), F32),
                pltpu.VMEM((blocks * heads, SUB, SUB), F32),
                pltpu.VMEM((blocks * heads, 8, SUB), F32),
                pltpu.VMEM((tokens, wv.shape[1]), F32),
                pltpu.VMEM((tokens, wv.shape[1]), BF16),
                pltpu.VMEM((heads, 2 * SUB, SUB), F32),
                pltpu.VMEM((heads, 2 * SUB + 16, SUB), BF16),
                pltpu.VMEM((heads, 2 * SUB + 16, SUB), BF16),
                pltpu.VMEM((heads // 2, slices, SUB + 16 + slab, SUB), BF16),
                pltpu.VMEM((n_chip, SUB + 16 + slab, SUB), BF16),
                pltpu.VMEM((n_chip, slab, SUB), BF16),
                pltpu.VMEM((heads, SUB, SUB), BF16),
                pltpu.VMEM((SUB, SUB), F32),
                dma((10,)),
                dma((4,)),
                dma((2, 2 * blocks, n_head // 2)),
                dma((2, n_head // 2 + 1)),
                dma((4,)),
                dma((n_chip,)),
                dma((1,)),
            ],
            compiler_params=pltpu.CompilerParams(
                collective_id=0, has_side_effects=True, vmem_limit_bytes=60 * 2**20
            ),
        )(hidden, wq, wk, wv, cq, ck, cv, gate, beta, init)

    return jax.shard_map(
        body,
        mesh=mesh,
        in_specs=(
            P("seq", "head"),
            P(None, "head"),
            P(None, "head"),
            P(None, "head"),
            P(None, "head"),
            P(None, "head"),
            P(None, "head"),
            P("head", "seq"),
            P("head", "seq"),
            P("head", None, None),
        ),
        out_specs=(P("seq", "head"), P("seq", "head", None, None)),
        check_vma=False,
    )
```

```python
import functools

import jax
import jax.numpy as jnp
from jax import lax
from jax.experimental import pallas as pl
from jax.experimental.pallas import tpu as pltpu
from jax.sharding import PartitionSpec as P

MESH = pl.DeviceIdType.MESH
F32 = jnp.float32
BF16 = jnp.bfloat16
SUB = 128
HALO = 16
LEVELS = (2, 4, 8, 16, 32, 64)
FIRST = (
    (0, 0, 0), (0, 1, 0), (1, 0, 0), (2, 1, 0), (3, 0, 0), (2, 0, 0), (0, 0, 1),
    (1, 1, 0), (1, 0, 1), (2, 1, 1), (3, 1, 0), (0, 1, 1), (0, 0, 2), (1, 1, 1),
    (1, 0, 2), (3, 0, 1), (2, 0, 1), (0, 1, 2), (0, 0, 3), (3, 1, 1), (1, 1, 2),
    (1, 0, 3), (2, 0, 2), (3, 0, 2), (2, 1, 2),
)
BESIDE = ((2, 3, 1, 2), (5, 2, 0, 3), (5, 3, 0, 3),)
HALO_AFTER = (5, 10, 15, 20)
NT = (((1,), (1,)), ((), ()))


def mm(left, right):
    return jnp.dot(left, right, preferred_element_type=F32)


def mm_nt(left, right):
    return lax.dot_general(left, right, NT, preferred_element_type=F32)


def split3(value):
    high = value.astype(BF16).astype(F32)
    mid = (value - high).astype(BF16).astype(F32)
    low = value - high - mid
    row = lax.broadcasted_iota(jnp.int32, (16, SUB), 0)
    tile = jnp.where(row == 0, high, jnp.where(row == 1, mid, jnp.where(row == 2, low, 0.0)))
    return tile.astype(BF16)


def joined3(tile):
    return jnp.sum(tile.astype(F32), axis=0, keepdims=True)


def kernel(
    n_seq,
    n_head,
    hidden_ref,
    wq_ref,
    wk_ref,
    wv_ref,
    cq_hbm,
    ck_hbm,
    cv_hbm,
    gate_hbm,
    beta_hbm,
    init_hbm,
    core_ref,
    closing_ref,
    gbuf,
    w_ref,
    gate_ref,
    beta_ref,
    init_ref,
    cq_ref,
    ck_ref,
    cv_ref,
    x_ref,
    tap_ref,
    mask_ref,
    state_ref,
    decay_ref,
    decays_ref,
    factor_ref,
    retain_ref,
    beta_full,
    both_full,
    rows_ref,
    partial_ref,
    reach_ref,
    total_ref,
    tx0,
    rx0,
    tx1,
    rx1,
    tx2,
    inc_ref,
    initt_ref,
    local_sem,
    sent_sem,
    ring_recv,
    halo_sem,
    pair_sem,
    a_recv,
    b_recv,
):
    tokens = hidden_ref.shape[0]
    width = hidden_ref.shape[1]
    blocks = tokens // SUB
    heads = gate_hbm.shape[0]
    qcols = wq_ref.shape[1]
    n_chip = n_seq // 2
    me_s = lax.axis_index("seq")
    me_h = lax.axis_index("head")
    core = lax.rem(me_s, 2)
    chip = lax.div(me_s, 2)
    partner = me_s + 1 - 2 * core
    right = lax.rem(me_h + 1, n_head)
    left = lax.rem(me_h + n_head - 1, n_head)

    barrier = pltpu.get_barrier_semaphore()
    for neighbour in (left, right):
        pl.semaphore_signal(
            barrier, inc=1, device_id={"seq": me_s, "head": neighbour}, device_id_type=MESH
        )
    later = lax.rem(me_s + 1, n_seq)

    def greet(i, carry):
        @pl.when(i != me_s)
        def _():
            pl.semaphore_signal(
                barrier, inc=1, device_id={"seq": i, "head": me_h}, device_id_type=MESH
            )

        return carry

    lax.fori_loop(0, n_seq, greet, 0)

    own_columns = pl.ds(pl.multiple_of(me_h * width, width), width)
    own_copy = pltpu.make_async_copy(
        hidden_ref, gbuf.at[pl.ds(0, tokens), own_columns], local_sem.at[0]
    )
    own_copy.start()
    loads = []
    for source, target in (
        (wq_ref, w_ref.at[:, pl.ds(0, qcols)]),
        (wk_ref, w_ref.at[:, pl.ds(qcols, qcols)]),
        (wv_ref, w_ref.at[:, pl.ds(2 * qcols, wv_ref.shape[1])]),
        (gate_hbm, gate_ref),
        (beta_hbm, beta_ref),
        (init_hbm, init_ref),
        (cq_hbm, cq_ref),
        (ck_hbm, ck_ref),
        (cv_hbm, cv_ref),
    ):
        loads.append(pltpu.make_async_copy(source, target, local_sem.at[1 + len(loads)]))
        loads[-1].start()

    row = lax.broadcasted_iota(jnp.int32, (SUB, SUB), 0)
    col = lax.broadcasted_iota(jnp.int32, (SUB, SUB), 1)
    for index, size in enumerate(LEVELS):
        here = (lax.div(row, 2 * size) == lax.div(col, 2 * size)) & (
            lax.div(row, size) > lax.div(col, size)
        )
        mask_ref[index] = jnp.where(here, 1.0, 0.0).astype(BF16)
    pairs = (lax.div(row, 2) == lax.div(col, 2)) & (row > col)
    mask_ref[len(LEVELS)] = jnp.where(pairs, 1.0, 0.0).astype(BF16)
    mask_ref[len(LEVELS) + 1] = jnp.where(row == col, 1.0, 0.0).astype(BF16)
    state_ref[...] = jnp.zeros_like(state_ref)
    decay_ref[...] = jnp.ones_like(decay_ref)

    own_copy.wait()
    pl.semaphore_wait(barrier, n_seq - 1 + 2)

    part_rows = SUB // 2

    def hop(way, chunk, which, back):
        owner = lax.rem(me_h + (n_head - back if way == 0 else back), n_head)
        part = way + which - 2 * way * which
        rows = pl.ds(pl.multiple_of(chunk * SUB + part * part_rows, part_rows), part_rows)
        place = gbuf.at[rows, pl.ds(pl.multiple_of(owner * width, width), width)]
        return pltpu.make_async_remote_copy(
            src_ref=place,
            dst_ref=place,
            send_sem=sent_sem.at[0],
            recv_sem=ring_recv.at[way, 2 * chunk + which, back],
            device_id={"seq": me_s, "head": right if way == 0 else left},
            device_id_type=MESH,
        )

    def event(chunk, which, back):
        for way in (0, 1):
            if isinstance(back, int):
                if back:
                    hop(way, chunk, which, back - 1).wait_recv()
            else:

                @pl.when(back > 0)
                def _():
                    hop(way, chunk, which, back - 1).wait_recv()

            hop(way, chunk, which, back).start()

    def service(pair, stage):
        entries = [entry[1:] for entry in BESIDE if entry[0] == stage]
        if entries:

            if pair == 0:
                for entry in entries:
                    event(*entry)

    def arrived(chunk):
        for way in (0, 1):
            hop(way, chunk, 0, 3).wait_recv()
            hop(way, chunk, 1, 2).wait_recv()

    halo_first = pltpu.make_async_remote_copy(
        src_ref=gbuf.at[pl.ds(tokens - HALO, HALO), own_columns],
        dst_ref=gbuf.at[pl.ds(tokens, HALO), own_columns],
        send_sem=sent_sem.at[1],
        recv_sem=halo_sem.at[0, n_head // 2],
        device_id={"seq": later, "head": me_h},
        device_id_type=MESH,
    )

    def halo_hop(way, back):
        owner = lax.rem(me_h + (n_head - back if way == 0 else back), n_head)
        place = gbuf.at[
            pl.ds(tokens, HALO), pl.ds(pl.multiple_of(owner * width, width), width)
        ]
        return pltpu.make_async_remote_copy(
            src_ref=place,
            dst_ref=place,
            send_sem=sent_sem.at[1],
            recv_sem=halo_sem.at[way, back],
            device_id={"seq": me_s, "head": right if way == 0 else left},
            device_id_type=MESH,
        )

    def halo_event(back):
        if back == 0:
            halo_first.wait_recv()
        for way in (0, 1):
            if back:
                halo_hop(way, back - 1).wait_recv()
            if back < n_head // 2 - way:
                halo_hop(way, back).start()

    on_or_below = row >= col
    below = row > col

    def prepare(n):
        at = slice(SUB * n, SUB * n + SUB)
        gates = gate_ref[:, at]
        along = jnp.dot(
            jnp.concatenate([gates, gates], axis=0),
            jnp.where(row <= col, 1.0, 0.0),
            precision=lax.Precision.HIGHEST,
            preferred_element_type=F32,
        )[:heads]
        columns8 = jnp.concatenate([along, beta_ref[:, at]], axis=0).T
        for h in range(heads):
            index = n * heads + h
            c_row, c_end = along[h : h + 1, :], along[h : h + 1, SUB - 1 :]
            c_col = columns8[:, h : h + 1]
            b_col = columns8[:, heads + h : heads + h + 1]
            retain = jnp.exp(c_col)
            decay = jnp.exp(jnp.where(on_or_below, c_col - c_row, -1e30))
            decays_ref[index] = decay
            factor_ref[index] = jnp.where(below, decay, 0.0) * b_col
            retain_ref[index] = jnp.broadcast_to(retain, (SUB, SUB))
            beta_full[index] = jnp.broadcast_to(b_col, (SUB, SUB))
            both_full[index] = jnp.broadcast_to(b_col * retain, (SUB, SUB))
            rows_ref[index, 0:1] = jnp.exp(c_end - c_row)
            rows_ref[index, 1:2] = jnp.broadcast_to(jnp.exp(c_end), (1, SUB))

    halo_bytes = gbuf.at[pl.ds(tokens, HALO)]

    def project(start, size, place, columns=slice(None)):
        rows = gbuf[pl.ds(start, size), :]
        x_ref[pl.ds(place, size), columns] = mm(rows, w_ref[:, columns]).astype(BF16).astype(F32)

    def owner_columns(steps):
        return [
            pl.ds(pl.multiple_of(lax.rem(me_h + step, n_head) * width, width), width)
            for step in steps
        ]

    def gathered(start, size, columns):
        return jnp.concatenate([gbuf[pl.ds(start, size), c] for c in columns], axis=1)

    def weights(owners, columns):
        return jnp.concatenate([w_ref[c, columns] for c in owners], axis=0)

    def reach_of(n):
        return 2 if n < 2 else 1


    def project_near(n):
        reach = reach_of(n)
        owners = owner_columns(range(-reach + n_head, reach + n_head + 1))
        rows = gathered(n * SUB, SUB, owners)
        x_ref[pl.ds(n * SUB + HALO, SUB), :] = mm(rows, weights(owners, slice(None)))

    def project_far(n, start, place, columns):
        owners = owner_columns(range(reach_of(n) + 1, n_head - reach_of(n)))
        total = x_ref[pl.ds(place, SUB), columns] + mm(
            gathered(start, SUB, owners), weights(owners, columns)
        )
        x_ref[pl.ds(place, SUB), columns] = total.astype(BF16).astype(F32)

    def start_conv():
        tap_ref[:, :qcols] = cq_ref[...].astype(F32)
        tap_ref[:, qcols : 2 * qcols] = ck_ref[...].astype(F32)
        tap_ref[:, 2 * qcols :] = cv_ref[...].astype(F32)
        halo_hop(0, n_head // 2 - 1).wait_recv()
        project(tokens, HALO, 0)

        @pl.when(me_s == 0)
        def _():
            x_ref[:HALO] = jnp.zeros((HALO, x_ref.shape[1]), F32)

    for entry in FIRST[:2]:
        event(*entry)
    halo_first.start()
    for copy in loads:
        copy.wait()
    for index, entry in enumerate(FIRST[2:], 2):
        if index in (5, 9, 12, 15):
            prepare((5, 9, 12, 15).index(index))
        event(*entry)
        for n in range(blocks):
            hops = reach_of(n)
            if index == max(FIRST.index((n, 0, hops)), FIRST.index((n, 1, hops))):
                project_near(n)
        if index in HALO_AFTER:
            halo_event(HALO_AFTER.index(index))
    def conv(base, columns):
        total = None
        window = x_ref[pl.ds(base, SUB + HALO), columns]
        for tap in range(4):
            first = HALO - 3 + tap
            term = tap_ref[tap : tap + 1, columns] * window[first : first + SUB]
            total = term if total is None else total + term
        return (total * pl.reciprocal(1.0 + jnp.exp(-total), approx=True)).astype(BF16)

    def unit(value, factor):
        value = value.astype(F32)
        squares = jnp.sum(value * value, axis=1, keepdims=True)
        return (value * (lax.rsqrt(squares + 1e-06) * factor)).astype(BF16)

    per_key = heads // (qcols // SUB)

    def project_block(pair, stage, n):
        base = n * SUB
        arrived(n)
        for part in range(2):
            service(pair, stage + part)
            columns = slice(part * 2 * qcols, part * 2 * qcols + 2 * qcols)
            project_far(n, base, base + HALO, columns)

    def systems(n):
        base = n * SUB
        found = []
        for kh in range(qcols // SUB):
            at = slice(SUB * kh, SUB * kh + SUB)
            q = unit(conv(base, at), SUB**-0.5)
            k = unit(conv(base, slice(qcols + SUB * kh, qcols + SUB * kh + SUB)), 1.0)
            both = mm_nt(jnp.concatenate([k, q, mask_ref[len(LEVELS) + 1]], axis=0), k)
            k = k.astype(F32)
            k_t = both[2 * SUB :]
            for h in range(per_key * kh, per_key * kh + per_key):
                index = n * heads + h
                lower = factor_ref[index] * both[:SUB]
                mix = (decays_ref[index] * both[SUB : 2 * SUB]).astype(BF16)
                lower = lower.astype(BF16)
                start = mask_ref[len(LEVELS) + 1] - lower * mask_ref[len(LEVELS)]
                v = conv(base, slice(2 * qcols + SUB * h, 2 * qcols + SUB * h + SUB))
                right_side = jnp.concatenate(
                    [
                        (beta_full[index] * v.astype(F32)).astype(BF16),
                        (both_full[index] * k).astype(BF16),
                    ],
                    axis=1,
                )
                weighted = (k_t * rows_ref[index, 0:1]).astype(BF16)
                query = retain_ref[index] * q.astype(F32)
                found.append(
                    (
                        lower,
                        start,
                        right_side,
                        jnp.concatenate([mix, weighted], axis=0),
                        query,
                    )
                )
        return found

    def pair_step(pair, carry):
        found = []
        for n in (2 * pair, 2 * pair + 1):
            stage = 3 * (len(found) // heads)
            project_block(pair, stage, n)
            if stage == 0 and pair == 0:
                start_conv()
            service(pair, stage + 2)
            found += systems(n)
        lowers = [each[0] for each in found]
        solved = [each[1] for each in found]
        for index in range(len(LEVELS)):
            if index % 2 == 0:
                service(pair, 6 + index // 2)
            halves = [
                mm(t, low * mask_ref[index]).astype(BF16) for t, low in zip(solved, lowers)
            ]
            solved = [t - mm(x, t).astype(BF16) for t, x in zip(solved, halves)]
        updates = [mm(t, each[2]).astype(BF16) for t, each in zip(solved, found)]
        stacked = [mm(each[3], u) for u, each in zip(updates, found)]
        for second in range(2):
            n = 2 * pair + second
            here = pl.ds(n * SUB, SUB)
            for h in range(heads):
                both = stacked[heads * second + h]
                keep = rows_ref[n * heads + h, 1:2]
                query_eff = found[heads * second + h][4] - both[:SUB, SUB:]
                offset, correction = both[SUB:, :SUB], both[SUB:, SUB:]
                state = state_ref[h]
                so_far = decay_ref[h, 0:1]
                moved = mm(
                    jnp.concatenate([query_eff, correction], axis=0).astype(BF16),
                    state.astype(BF16),
                )
                at = slice(SUB * h, SUB * h + SUB)
                partial_ref[here, at] = both[:SUB, :SUB] + moved[:SUB, :SUB]
                reach_ref[here, at] = (so_far * query_eff - moved[:SUB, SUB:]).astype(BF16)
                state_ref[h, :, :SUB] = keep * state[:, :SUB] - moved[SUB:, :SUB] + offset
                state_ref[h, :, SUB:] = (
                    keep * state[:, SUB:] + so_far * correction - moved[SUB:, SUB:]
                )
                decay_ref[h] = decay_ref[h] * keep
        return carry

    for pair in range(blocks // 2):
        pair_step(pair, 0)

    for h in range(heads):
        total_ref[h, :SUB] = state_ref[h, :, SUB:].T
        total_ref[h, SUB:] = state_ref[h, :, :SUB].T
        tx0[h, :SUB] = total_ref[h, :SUB].astype(BF16)
        tx0[h, SUB : SUB + 16] = split3(decay_ref[h, 0:1, :])
        tx0[h, SUB + 16 :] = total_ref[h, SUB:].astype(BF16)
    own_heads = heads // 2

    def swap(which):
        mine = pl.ds((core if which else 1 - core) * own_heads, own_heads)
        return pltpu.make_async_remote_copy(
            src_ref=tx0.at[mine],
            dst_ref=rx0.at[mine],
            send_sem=pair_sem.at[which],
            recv_sem=pair_sem.at[2 + which],
            device_id={"seq": partner, "head": me_h},
            device_id_type=MESH,
        )

    swap(0).start()
    swap(1).start()
    swap(0).wait_recv()

    slices = n_chip // heads
    slab = SUB // slices
    def job(q):
        part = lax.div(q, heads)
        head = lax.rem(part + q, heads)
        return part, head

    def to_handler(q):
        part, head = job(q)
        return pltpu.make_async_remote_copy(
            src_ref=tx1.at[lax.rem(head, own_heads), part],
            dst_ref=rx1.at[chip],
            send_sem=sent_sem.at[2],
            recv_sem=a_recv.at[chip],
            device_id={"seq": 2 * q + core, "head": me_h},
            device_id_type=MESH,
        )

    def for_me(q):
        return lax.div(job(q)[1], own_heads) == core

    def send_a(i, k, carry):
        q = chip ^ k

        @pl.when((q != chip) & (job(q)[1] == core * own_heads + i))
        def _():
            to_handler(q).start()

        return carry

    for i in range(own_heads):
        h = core * own_heads + i
        mine, other = tx0[h], rx0[h]
        flag = (jnp.zeros((1, 1), jnp.int32) + core) == 0
        early = jnp.where(flag, mine.astype(F32), other.astype(F32))
        late = jnp.where(flag, other.astype(F32), mine.astype(F32))
        g0 = joined3(early[SUB : SUB + 16])
        g1 = joined3(late[SUB : SUB + 16])
        c0, s0 = early[:SUB], early[SUB + 16 :]
        c1, s1 = late[:SUB], late[SUB + 16 :]
        moved = mm(jnp.concatenate([c0, s0], axis=0).astype(BF16), c1.astype(BF16))
        c_new = (g1 * c0 + g0 * c1 - moved[:SUB]).astype(BF16)
        s_new = (g1 * s0 + s1 - moved[SUB:]).astype(BF16)
        g_new = split3(g0 * g1)
        for part in range(slices):
            tx1[i, part, :SUB] = c_new
            tx1[i, part, SUB : SUB + 16] = g_new
            tx1[i, part, SUB + 16 :] = s_new[slab * part : slab * part + slab]
        lax.fori_loop(0, n_chip, functools.partial(send_a, i), 0)

    my_part, my_head = job(chip)
    handling = for_me(chip)

    def from_handler(q):
        part, head = job(q)
        return inc_ref.at[head, pl.ds(pl.multiple_of(part * slab, slab), slab)]

    def hand_on(i, other_core):
        return pltpu.make_async_remote_copy(
            src_ref=tx2.at[i],
            dst_ref=from_handler(chip),
            send_sem=sent_sem.at[3],
            recv_sem=b_recv.at[0],
            device_id={"seq": 2 * i + other_core, "head": me_h},
            device_id_type=MESH,
        )

    @pl.when(handling)
    def _():
        rx1[chip] = tx1[lax.rem(my_head, own_heads), my_part]
        initt_ref[...] = init_ref[my_head].T
        state0 = initt_ref[pl.ds(pl.multiple_of(my_part * slab, slab), slab)]

        def chain(i, state):
            tx2[i] = state.astype(BF16)
            for other_core in (0, 1):

                @pl.when(2 * i + other_core != me_s)
                def _():
                    hand_on(i, other_core).start()

            @pl.when(i != chip)
            def _():
                pltpu.make_async_remote_copy(
                    src_ref=tx1.at[0, 0],
                    dst_ref=rx1.at[i],
                    send_sem=sent_sem.at[2],
                    recv_sem=a_recv.at[i],
                    device_id={"seq": partner, "head": me_h},
                    device_id_type=MESH,
                ).wait_recv()

            message = rx1[i]
            moved = mm(state.astype(BF16), message[:SUB])
            keep = joined3(message[SUB : SUB + 16])
            return keep * state - moved + message[SUB + 16 :].astype(F32)

        lax.fori_loop(0, n_chip, chain, state0)
        inc_ref[my_head, pl.ds(pl.multiple_of(my_part * slab, slab), slab)] = tx2[chip]

    @pl.when(handling)
    def _():
        b_bytes = reach_ref.at[pl.ds(0, (n_chip - 1) * slab), pl.ds(0, SUB)]
        pltpu.make_async_copy(b_bytes, b_bytes, b_recv.at[0]).wait()

    @pl.when(jnp.logical_not(handling))
    def _():
        b_bytes = inc_ref
        pltpu.make_async_copy(b_bytes, b_bytes, b_recv.at[0]).wait()

    swap(1).wait_recv()
    for h in range(heads):
        came = inc_ref[h].astype(F32)
        first = rx0[h]
        stepped = (
            joined3(first[SUB : SUB + 16]) * came
            - mm(inc_ref[h], first[:SUB])
            + first[SUB + 16 :].astype(F32)
        )
        flag = (jnp.zeros((1, 1), jnp.int32) + core) == 0
        came = jnp.where(flag, came, stepped)
        at = slice(SUB * h, SUB * h + SUB)
        short = came.astype(BF16)
        core_ref[:, at] = (partial_ref[:, at] + mm_nt(reach_ref[:, at], short)).astype(BF16)
        total = total_ref[h]
        closing = (
            decay_ref[h, 0:1, :] * came - mm(short, total[:SUB].astype(BF16)) + total[SUB:]
        )
        closing_ref[0, h] = closing.T

    swap(0).wait_send()
    swap(1).wait_send()
    ring_bytes = gbuf.at[pl.ds(0, tokens), pl.ds(0, (n_head - 1) * width)]
    pltpu.make_async_copy(ring_bytes, ring_bytes, sent_sem.at[0]).wait()
    pltpu.make_async_copy(halo_bytes, halo_bytes, sent_sem.at[1]).wait()

    messages = n_chip // 2

    @pl.when(handling)
    def _():
        a_bytes = rx1.at[pl.ds(0, messages - 1)]
        pltpu.make_async_copy(a_bytes, a_bytes, sent_sem.at[2]).wait()
        b_bytes = gbuf.at[pl.ds(0, (n_seq - 1) * slab // 2), pl.ds(0, 2 * SUB)]
        pltpu.make_async_copy(b_bytes, b_bytes, sent_sem.at[3]).wait()

    @pl.when(jnp.logical_not(handling))
    def _():
        a_bytes = rx1.at[pl.ds(0, messages)]
        pltpu.make_async_copy(a_bytes, a_bytes, sent_sem.at[2]).wait()


def solution(mesh):
    n_seq, n_head = mesh.shape["seq"], mesh.shape["head"]
    n_chip = n_seq // 2

    def body(hidden, wq, wk, wv, cq, ck, cv, gate, beta, init):
        tokens, width = hidden.shape
        heads = gate.shape[0]
        columns = wq.shape[1] + wk.shape[1] + wv.shape[1]
        slices = n_chip // heads
        slab = SUB // slices
        blocks = tokens // SUB
        vmem = pl.BlockSpec(memory_space=pltpu.VMEM)
        hbm = pl.BlockSpec(memory_space=pltpu.HBM)
        dma = pltpu.SemaphoreType.DMA
        return pl.pallas_call(
            functools.partial(kernel, n_seq, n_head),
            out_shape=(
                jax.ShapeDtypeStruct((tokens, wv.shape[1]), BF16),
                jax.ShapeDtypeStruct((1,) + init.shape, F32),
            ),
            in_specs=[hbm] * 10,
            out_specs=(vmem, vmem),
            scratch_shapes=[
                pltpu.VMEM((tokens + HALO, width * n_head), BF16),
                pltpu.VMEM((wq.shape[0], columns), BF16),
                pltpu.VMEM(gate.shape, F32),
                pltpu.VMEM(beta.shape, F32),
                pltpu.VMEM(init.shape, F32),
                pltpu.VMEM(cq.shape, BF16),
                pltpu.VMEM(ck.shape, BF16),
                pltpu.VMEM(cv.shape, BF16),
                pltpu.VMEM((tokens + HALO, columns), F32),
                pltpu.VMEM((4, columns), F32),
                pltpu.VMEM((len(LEVELS) + 2, SUB, SUB), BF16),
                pltpu.VMEM((heads, SUB, 2 * SUB), F32),
                pltpu.VMEM((heads, 8, SUB), F32),
                pltpu.VMEM((blocks * heads, SUB, SUB), F32),
                pltpu.VMEM((blocks * heads, SUB, SUB), F32),
                pltpu.VMEM((blocks * heads, SUB, SUB), F32),
                pltpu.VMEM((blocks * heads, SUB, SUB), F32),
                pltpu.VMEM((blocks * heads, SUB, SUB), F32),
                pltpu.VMEM((blocks * heads, 8, SUB), F32),
                pltpu.VMEM((tokens, wv.shape[1]), F32),
                pltpu.VMEM((tokens, wv.shape[1]), BF16),
                pltpu.VMEM((heads, 2 * SUB, SUB), F32),
                pltpu.VMEM((heads, 2 * SUB + 16, SUB), BF16),
                pltpu.VMEM((heads, 2 * SUB + 16, SUB), BF16),
                pltpu.VMEM((heads // 2, slices, SUB + 16 + slab, SUB), BF16),
                pltpu.VMEM((n_chip, SUB + 16 + slab, SUB), BF16),
                pltpu.VMEM((n_chip, slab, SUB), BF16),
                pltpu.VMEM((heads, SUB, SUB), BF16),
                pltpu.VMEM((SUB, SUB), F32),
                dma((10,)),
                dma((4,)),
                dma((2, 2 * blocks, n_head // 2)),
                dma((2, n_head // 2 + 1)),
                dma((4,)),
                dma((n_chip,)),
                dma((1,)),
            ],
            compiler_params=pltpu.CompilerParams(
                collective_id=0, has_side_effects=True, vmem_limit_bytes=60 * 2**20
            ),
        )(hidden, wq, wk, wv, cq, ck, cv, gate, beta, init)

    return jax.shard_map(
        body,
        mesh=mesh,
        in_specs=(
            P("seq", "head"),
            P(None, "head"),
            P(None, "head"),
            P(None, "head"),
            P(None, "head"),
            P(None, "head"),
            P(None, "head"),
            P("head", "seq"),
            P("head", "seq"),
            P("head", None, None),
        ),
        out_specs=(P("seq", "head"), P("seq", "head", None, None)),
        check_vma=False,
    )
```
